32 devices in a mesh: groups: 2 (over y), tok: 16 (over z, x, core).
Axes of the slice: x: 2, y: 2, z: 4, core: 2. Of those that a mesh axis runs over, the one named last changes fastest.
Arguments:
- query_rows: bfloat16 [8192, 768], P(('groups', 'tok')), parts along dimension 0, may hold values from -6 to 6
- key_rows: bfloat16 [8192, 768], P(('groups', 'tok')), parts along dimension 0, may hold values from -6 to 6
- value_rows: bfloat16 [8192, 768], P(('groups', 'tok')), parts along dimension 0, may hold values from -6 to 6
- out_rows: bfloat16 [8192, 768], P(('groups', 'tok')), parts along dimension 0, may hold values from -6 to 6
- grad_out: bfloat16 [8192, 768], P(('groups', 'tok')), parts along dimension 0, may hold values from -6 to 6
- normalizer: float32 [16, 8192], P(None, ('groups', 'tok')), parts along dimension 1, may hold values from 3 to 5
- keep_tasks: int32 [32, 5], P('groups'), parts along dimension 0, may hold values from 0 to 1, as said below
Outputs:
- grad_query: bfloat16 [8192, 768], P(('groups', 'tok')), parts along dimension 0
- grad_key: bfloat16 [8192, 768], P(('groups', 'tok')), parts along dimension 0
- grad_value: bfloat16 [8192, 768], P(('groups', 'tok')), parts along dimension 0
The draws below stay inside these ranges and needn't reach their ends.
There are 2 independent parts, one for each index of `groups`. The reference program is written for one: setup_inputs(seed, part) draws one part's arguments, and reference() takes and returns one part's arrays. A program takes and returns all parts, laid end to end along the dimension named above; each array names one. Nothing has to cross between parts.
Inputs may be any that keep to these rules, and one draw needn't show every extreme that they name: keep_tasks[a, 2] = 1 for every block a; entries naming a key block outside 0 to 15 are ignored.
All inputs are finite; a program needn't handle non-finite values.
Results may differ from the reference program's by a relative error of at most 0.0053.
Values may be sent and summed in bfloat16 or wider, within the bound.
No kernel may reach another device: no remote copies, remote signals or barrier semaphores. Data moves between devices by JAX's collectives and lax.ppermute only.
A program may use at most 128 MiB of HBM per device.

```python
import jax
import jax.numpy as jnp
from jax import lax

D = 768
HEADS = 16
BLOCK = 256
RADIUS = 2
WIN = 5
NBLK = 16
TOKENS = 4096


def draw_keep_tasks(key, part):
    first = jax.random.fold_in(key, 11)
    second = jax.random.fold_in(key, 23)
    density = jax.random.randint(first, (NBLK, 1), 0, 5)
    levels = jax.random.randint(second, (NBLK, WIN), 0, 4)
    column = jnp.arange(WIN)[None, :]
    keep = (levels < density) | (column == RADIUS)
    return jnp.where(keep, 1, 0).astype(jnp.int32)


def steps_of(own_key, dims, pieces, smallest, top_value):
    def one(axis_at, parts):
        heights = jax.random.uniform(jax.random.fold_in(jax.random.fold_in(own_key, 6), axis_at), (parts,), jnp.float32, smallest / len(pieces), top_value / len(pieces))
        return jnp.repeat(jnp.exp(heights), dims[axis_at] // parts).reshape((-1,) + (1,) * (len(dims) - axis_at - 1))

    gain = one(*pieces[0])
    for cut in pieces[1:]:
        gain = gain * one(*cut)
    return gain


def centred(rng, extent, spread, bound, shards=(), held_as=jnp.bfloat16):
    array = jax.random.normal(rng, extent, jnp.float32) * spread
    if len(shards) > 0:
        array = steps_of(rng, extent, shards, -0.22, 0.18) * array
    return jnp.clip(array, min=-bound, max=bound).astype(held_as)


def setup_inputs(seed: int = 0, part: int = 0) -> dict:
    key_list = jax.random.split(jax.random.key(seed), 8)
    own_keys = jax.random.split(jax.random.fold_in(key_list[7], part), 8)
    query_rows = centred(own_keys[0], (TOKENS, D), 1.0, 6.0, ((0, 16),))
    key_rows = centred(own_keys[1], (TOKENS, D), 1.0, 6.0, ((0, 16),))
    value_rows = centred(own_keys[2], (TOKENS, D), 1.0, 6.0, ((0, 16),))
    out_rows = centred(own_keys[3], (TOKENS, D), 1.0, 6.0, ((0, 16),))
    grad_out = centred(own_keys[4], (TOKENS, D), 1.0, 6.0, ((0, 16),))
    normalizer = jnp.clip(3.0 + 2.0 * jax.random.uniform(own_keys[5], (HEADS, TOKENS), jnp.float32) ** steps_of(own_keys[5], (HEADS, TOKENS), ((1, 16),), -0.2, 0.2), 3.0, 5.0)
    keep_tasks = draw_keep_tasks(jax.random.fold_in(jax.random.fold_in(key_list[7], part), 71), part)
    return dict(query_rows=query_rows, key_rows=key_rows, value_rows=value_rows, out_rows=out_rows, grad_out=grad_out, normalizer=normalizer, keep_tasks=keep_tasks)


def task_grads(q_block, dout_block, lse_block, delta_block, k_block, v_block, scale):
    scores = jnp.einsum('qhe,khe->hqk', q_block, k_block) * scale
    probs = jnp.exp(scores - lse_block[:, :, None])
    prob_grad = jnp.einsum('qhe,khe->hqk', dout_block, v_block)
    score_grad = lax.optimization_barrier((probs * (prob_grad - delta_block[:, :, None])).astype(jnp.bfloat16)).astype(jnp.float32)
    probs_low = lax.optimization_barrier(probs.astype(jnp.bfloat16)).astype(jnp.float32)
    term_q = jnp.einsum('hqk,khe->qhe', score_grad, k_block) * scale
    term_k = jnp.einsum('hqk,qhe->khe', score_grad, q_block) * scale
    term_v = jnp.einsum('hqk,qhe->khe', probs_low, dout_block)
    return term_q, term_k, term_v


def reference(query_rows, key_rows, value_rows, out_rows, grad_out, normalizer, keep_tasks):
    width = query_rows.shape[1]
    head_dim = width // HEADS
    scale = head_dim ** -0.5
    shape4 = (NBLK, BLOCK, HEADS, head_dim)
    q_all = query_rows.astype(jnp.float32).reshape(shape4)
    k_all = key_rows.astype(jnp.float32).reshape(shape4)
    v_all = value_rows.astype(jnp.float32).reshape(shape4)
    o_all = out_rows.astype(jnp.float32).reshape(shape4)
    g_all = grad_out.astype(jnp.float32).reshape(shape4)
    delta = jnp.transpose(jnp.sum(g_all * o_all, axis=3), (0, 2, 1))
    lse_all = jnp.transpose(normalizer.astype(jnp.float32).reshape(HEADS, NBLK, BLOCK), (1, 0, 2))
    padding = jnp.zeros((RADIUS, BLOCK, HEADS, head_dim), jnp.float32)
    k_pad = jnp.concatenate([padding, k_all, padding], axis=0)
    v_pad = jnp.concatenate([padding, v_all, padding], axis=0)
    zeros3 = jnp.zeros((BLOCK, HEADS, head_dim), jnp.float32)

    def step(carry, block):
        dk_pad, dv_pad = carry
        q_block = lax.dynamic_index_in_dim(q_all, block, 0, keepdims=False)
        g_block = lax.dynamic_index_in_dim(g_all, block, 0, keepdims=False)
        lse_block = lax.dynamic_index_in_dim(lse_all, block, 0, keepdims=False)
        d_block = lax.dynamic_index_in_dim(delta, block, 0, keepdims=False)
        dq = zeros3
        for j in range(WIN):
            target = block - RADIUS + j
            inside = (target >= 0) & (target < NBLK)
            flag = jnp.where(inside, keep_tasks[block, j], 0)
            slot = (block + j).astype(jnp.int32)
            k_block = lax.dynamic_index_in_dim(k_pad, slot, 0, keepdims=False)
            v_block = lax.dynamic_index_in_dim(v_pad, slot, 0, keepdims=False)

            def live(unused):
                return task_grads(q_block, g_block, lse_block, d_block, k_block, v_block, scale)

            def dead(unused):
                return zeros3, zeros3, zeros3

            term_q, term_k, term_v = lax.cond(flag > 0, live, dead, 0)
            dq = dq + term_q
            old_k = lax.dynamic_index_in_dim(dk_pad, slot, 0, keepdims=False)
            dk_pad = lax.dynamic_update_index_in_dim(dk_pad, old_k + term_k, slot, 0)
            old_v = lax.dynamic_index_in_dim(dv_pad, slot, 0, keepdims=False)
            dv_pad = lax.dynamic_update_index_in_dim(dv_pad, old_v + term_v, slot, 0)
        return (dk_pad, dv_pad), dq

    start = (jnp.zeros_like(k_pad), jnp.zeros_like(v_pad))
    (dk_pad, dv_pad), dq_all = lax.scan(step, start, jnp.arange(NBLK, dtype=jnp.int32))
    total = NBLK * BLOCK
    grad_query = dq_all.reshape(total, width).astype(jnp.bfloat16)
    grad_key = dk_pad[RADIUS:RADIUS + NBLK].reshape(total, width).astype(jnp.bfloat16)
    grad_value = dv_pad[RADIUS:RADIUS + NBLK].reshape(total, width).astype(jnp.bfloat16)
    return grad_query, grad_key, grad_value
```

```python
import functools
import math

import jax
import jax.numpy as jnp
from jax import lax
from jax.experimental import pallas as pl
from jax.experimental.pallas import tpu as pltpu
from jax.sharding import PartitionSpec as P

HEADS = 16
RADIUS = 2
WIN = 5
PARTS = 3
CHUNK_HEADS = (8, 8)
NN = (((1,), (0,)), ((), ()))
NT = (((1,), (1,)), ((), ()))
TN = (((0,), (0,)), ((), ()))
LOG2E = math.log2(math.e)
F32 = jnp.float32
BF16 = jnp.bfloat16
VMEM = pl.BlockSpec(memory_space=pltpu.VMEM)
SMEM = pl.BlockSpec(memory_space=pltpu.SMEM)


def dot(left, right, dims):
    return lax.dot_general(left, right, dims, preferred_element_type=F32)


def params():
    return pltpu.CompilerParams(vmem_limit_bytes=40 * 1024 * 1024)


def cost(flops, size):
    return pl.CostEstimate(flops=flops, bytes_accessed=size, transcendentals=0)


def split_parts(value):
    out = []
    for _ in range(PARTS):
        piece = value.astype(BF16)
        out.append(piece)
        value = value - piece.astype(F32)
    return out


def extra_rows(heads):
    return -(-2 * PARTS * heads // 16) * 16


def pack_queries(chunks, head_dim, q_ref, do_ref, o_ref, lse_ref, *out_refs):
    q_t = q_ref[...].T
    do_t = do_ref[...].T
    o_t = o_ref[...].T
    lse = lse_ref[...] * LOG2E
    first = 0
    for heads, out_ref in zip(chunks, out_refs):
        rows = heads * head_dim
        span = slice(first * head_dim, first * head_dim + rows)
        out_ref[:rows] = q_t[span]
        out_ref[rows : 2 * rows] = do_t[span]
        product = do_t[span].astype(F32) * o_t[span].astype(F32)
        delta = jnp.concatenate(
            [
                jnp.sum(product[h * head_dim : (h + 1) * head_dim], axis=0, keepdims=True)
                for h in range(heads)
            ],
            axis=0,
        )
        pieces = split_parts(jnp.concatenate([lse[first : first + heads], delta], axis=0))
        pad = extra_rows(heads) - 2 * PARTS * heads
        if pad:
            pieces.append(jnp.zeros((pad, lse.shape[1]), BF16))
        joined = jnp.concatenate([piece.astype(F32) for piece in pieces], axis=0)
        out_ref[2 * rows :] = joined.astype(BF16)
        first += heads


def pack_keys(chunks, head_dim, k_ref, v_ref, *out_refs):
    k_t = k_ref[...].T
    v_t = v_ref[...].T
    first = 0
    for heads, out_ref in zip(chunks, out_refs):
        rows = heads * head_dim
        span = slice(first * head_dim, first * head_dim + rows)
        out_ref[:rows] = k_t[span]
        out_ref[rows:] = v_t[span]
        first += heads


def read_queries(x_ref, heads, head_dim):
    rows = heads * head_dim
    q = [x_ref[h * head_dim : (h + 1) * head_dim] for h in range(heads)]
    do = [x_ref[rows + h * head_dim : rows + (h + 1) * head_dim] for h in range(heads)]
    extra = x_ref[2 * rows :].astype(F32)
    step = 2 * heads
    total = extra[:step]
    for i in range(1, PARTS):
        total = total + extra[i * step : (i + 1) * step]
    lse = [total[h : h + 1] for h in range(heads)]
    delta = [total[heads + h : heads + h + 1] for h in range(heads)]
    return q, do, lse, delta


def read_keys(ref, heads, head_dim):
    rows = heads * head_dim
    k = [ref[h * head_dim : (h + 1) * head_dim] for h in range(heads)]
    v = [ref[rows + h * head_dim : rows + (h + 1) * head_dim] for h in range(heads)]
    return k, v


def task(queries, keys, factor):
    q, do, lse, delta = queries
    k, v = keys
    span = range(len(q))
    scores = [dot(k[i], q[i], TN) for i in span]
    prob_grad = [dot(v[i], do[i], TN) for i in span]
    probs = [jnp.exp2(scores[i] * factor - lse[i]) for i in span]
    score_grad = [(probs[i] * (prob_grad[i] - delta[i])).astype(BF16) for i in span]
    probs = [x.astype(BF16) for x in probs]
    dv = [dot(do[i], probs[i], NT) for i in span]
    dk = [dot(q[i], score_grad[i], NT) for i in span]
    dq = [dot(k[i], score_grad[i], NN) for i in span]
    return dq, dk, dv


def join(parts):
    return jnp.concatenate(parts, axis=0)


def flag_of(keep_ref, count, query, key):
    offset = key - query + RADIUS
    inside = (key >= 0) & (key < count) & (offset >= 0) & (offset < WIN)
    value = keep_ref[query, jnp.clip(offset, 0, WIN - 1)]
    return inside & (value > 0)


def own_kernel(heads, head_dim, factor, count, keep_ref, place_ref, x_ref, kv_ref, pkv_ref,
               dq_ref, dkv_ref, pdkv_ref):
    place = place_ref[0]
    partner = place + 1 - 2 * lax.rem(place, 2)
    queries = read_queries(x_ref, heads, head_dim)
    dq, dk, dv = task(queries, read_keys(kv_ref, heads, head_dim), factor)
    dq_ref[...] = join(dq)
    dkv_ref[...] = join(dk + dv)
    flag = flag_of(keep_ref, count, place, partner)

    @pl.when(flag)
    def _():
        dq, dk, dv = task(queries, read_keys(pkv_ref, heads, head_dim), factor)
        dq_ref[...] += join(dq)
        pdkv_ref[...] = join(dk + dv).astype(BF16)

    @pl.when(jnp.logical_not(flag))
    def _():
        pdkv_ref[...] = jnp.zeros_like(pdkv_ref)


def far_kernel(heads, head_dim, factor, count, keep_ref, place_ref, x_ref, kv_ref, pkv_ref,
               fkv_ref, zkv_ref, dq_ref, dkv_ref, sdkv_ref, zdkv_ref, acc_ref):
    place = place_ref[0]
    spot = lax.rem(place, 4)
    low = spot < 2
    outer = (spot == 0) | (spot == 3)
    partner = place + 1 - 2 * lax.rem(place, 2)
    query = jnp.where(low, place + 2, place - 2)
    jump = jnp.where(low, 4, -4)
    queries = read_queries(x_ref, heads, head_dim)
    acc_ref[...] = jnp.zeros_like(acc_ref)

    def run(flag, load, out_ref):
        @pl.when(flag)
        def _():
            dq, dk, dv = task(queries, load(), factor)
            acc_ref[...] += join(dq)
            out_ref[...] = join(dk + dv).astype(out_ref.dtype)

        @pl.when(jnp.logical_not(flag))
        def _():
            out_ref[...] = jnp.zeros_like(out_ref)

    def side():
        k_p, v_p = read_keys(pkv_ref, heads, head_dim)
        k_f, v_f = read_keys(fkv_ref, heads, head_dim)
        pick = lambda a, b: jnp.where(outer, a, b)
        return [pick(a, b) for a, b in zip(k_p, k_f)], [pick(a, b) for a, b in zip(v_p, v_f)]

    side_key = jnp.where(outer, partner, partner + jump)
    run(flag_of(keep_ref, count, query, place), lambda: read_keys(kv_ref, heads, head_dim), dkv_ref)
    run(flag_of(keep_ref, count, query, side_key), side, sdkv_ref)
    run(
        flag_of(keep_ref, count, query, place + jump),
        lambda: read_keys(zkv_ref, heads, head_dim),
        zdkv_ref,
    )
    dq_ref[...] = acc_ref[...].astype(BF16)


def finish_kernel(chunks, head_dim, scale, *refs):
    ins, outs = refs[:-3], refs[-3:]
    groups = [ins[i * 7 : (i + 1) * 7] for i in range(len(chunks))]
    dq_all, dk_all, dv_all = [], [], []
    for heads, group in zip(chunks, groups):
        dq_own, dq_far, dkv_own, dkv_far, pdkv, sdkv, zdkv = group
        rows = heads * head_dim
        total = dkv_own[...] + dkv_far[...]
        for ref in (pdkv, sdkv, zdkv):
            total = total + ref[...].astype(F32)
        dq_all.append(((dq_own[...] + dq_far[...].astype(F32)) * scale).astype(BF16))
        dk_all.append((total[:rows] * scale).astype(BF16))
        dv_all.append(total[rows:].astype(BF16))
    for parts, ref in zip((dq_all, dk_all, dv_all), outs):
        ref[...] = join(parts).T


def per_device(query_rows, key_rows, value_rows, out_rows, grad_out, normalizer, keep_tasks):
    tokens, width = query_rows.shape
    head_dim = width // HEADS
    scale = head_dim ** (-0.5)
    factor = scale * LOG2E
    count = lax.axis_size("tok")
    chunks = CHUNK_HEADS
    place = jnp.reshape(lax.axis_index("tok"), (1,)).astype(jnp.int32)

    def send(value, pairs):
        pairs = [(a, b) for a, b in pairs if 0 <= b < count]
        return lax.ppermute(value, "tok", pairs)

    everyone = range(count)
    across = [(i, i ^ 2) for i in everyone]
    core = [(i, i ^ 1) for i in everyone]
    level_in = [(i, i - 4 if i % 4 < 2 else i + 4) for i in everyone]
    level_out = [(i, i + 4 if i % 4 < 2 else i - 4) for i in everyone]
    forward = [(i, i ^ 1) for i in everyone if i % 4 in (0, 3)]
    side_out = [(i, {0: i + 1, 1: i + 3, 2: i - 3, 3: i - 1}[i % 4]) for i in everyone]

    def shape(rows, dtype):
        return jax.ShapeDtypeStruct((rows, tokens), dtype)

    x_own = pl.pallas_call(
        functools.partial(pack_queries, chunks, head_dim),
        out_shape=[shape(2 * h * head_dim + extra_rows(h), BF16) for h in chunks],
        in_specs=[VMEM] * 4,
        out_specs=[VMEM] * len(chunks),
        compiler_params=params(),
        name="pack_queries",
    )(query_rows, grad_out, out_rows, normalizer)
    kv_own = pl.pallas_call(
        functools.partial(pack_keys, chunks, head_dim),
        out_shape=[shape(2 * h * head_dim, BF16) for h in chunks],
        in_specs=[VMEM] * 2,
        out_specs=[VMEM] * len(chunks),
        compiler_params=params(),
        name="pack_keys",
    )(key_rows, value_rows)
    x_far = [send(x, across) for x in x_own]
    kv_level = [send(kv, level_in) for kv in kv_own]
    kv_core = [send(kv, core) for kv in kv_own]
    kv_forward = [send(kv, forward) for kv in kv_level]

    finish_args = []
    for c, heads in enumerate(chunks):
        rows = heads * head_dim
        work = 10 * tokens * tokens * 256 * heads
        dq_own, dkv_own, pdkv = pl.pallas_call(
            functools.partial(own_kernel, heads, head_dim, factor, count),
            out_shape=[shape(rows, F32), shape(2 * rows, F32), shape(2 * rows, BF16)],
            in_specs=[SMEM] * 2 + [VMEM] * 3,
            out_specs=[VMEM] * 3,
            compiler_params=params(),
            cost_estimate=cost(2 * work, 8 * rows * tokens * 2),
            name="own_tasks",
        )(keep_tasks, place, x_own[c], kv_own[c], kv_core[c])
        dq_far, dkv_far, sdkv, zdkv = pl.pallas_call(
            functools.partial(far_kernel, heads, head_dim, factor, count),
            out_shape=[shape(rows, BF16), shape(2 * rows, F32), shape(2 * rows, BF16), shape(2 * rows, BF16)],
            in_specs=[SMEM] * 2 + [VMEM] * 5,
            out_specs=[VMEM] * 4,
            scratch_shapes=[pltpu.VMEM((rows, tokens), F32)],
            compiler_params=params(),
            cost_estimate=cost(3 * work, 16 * rows * tokens * 2),
            name="far_tasks",
        )(keep_tasks, place, x_far[c], kv_own[c], kv_core[c], kv_forward[c], kv_level[c])
        finish_args += [
            dq_own,
            send(dq_far, across),
            dkv_own,
            dkv_far,
            send(pdkv, core),
            send(sdkv, side_out),
            send(zdkv, level_out),
        ]
    grad_query, grad_key, grad_value = pl.pallas_call(
        functools.partial(finish_kernel, chunks, head_dim, scale),
        out_shape=[jax.ShapeDtypeStruct((tokens, width), BF16)] * 3,
        in_specs=[VMEM] * len(finish_args),
        out_specs=[VMEM] * 3,
        compiler_params=params(),
        name="finish",
    )(*finish_args)
    return grad_query, grad_key, grad_value


def solution(mesh):
    rows = P(("groups", "tok"), None)
    return jax.shard_map(
        per_device,
        mesh=mesh,
        in_specs=(rows, rows, rows, rows, rows, P(None, ("groups", "tok")), P("groups", None)),
        out_specs=(rows, rows, rows),
        check_vma=False,
    )
```

```python
import functools
import math

import jax
import jax.numpy as jnp
from jax import lax
from jax.experimental import pallas as pl
from jax.experimental.pallas import tpu as pltpu
from jax.sharding import PartitionSpec as P

HEADS = 16
RADIUS = 2
WIN = 5
PARTS = 3
CHUNK_HEADS = (8, 8)
NN = (((1,), (0,)), ((), ()))
NT = (((1,), (1,)), ((), ()))
TN = (((0,), (0,)), ((), ()))
LOG2E = math.log2(math.e)
F32 = jnp.float32
BF16 = jnp.bfloat16
VMEM = pl.BlockSpec(memory_space=pltpu.VMEM)
SMEM = pl.BlockSpec(memory_space=pltpu.SMEM)


def dot(left, right, dims):
    return lax.dot_general(left, right, dims, preferred_element_type=F32)


def join(parts):
    return jnp.concatenate(parts, axis=0)


def params():
    return pltpu.CompilerParams(vmem_limit_bytes=40 * 1024 * 1024)


def cost(flops, size):
    return pl.CostEstimate(flops=flops, bytes_accessed=size, transcendentals=0)


def split_parts(value):
    out = []
    for _ in range(PARTS):
        piece = value.astype(BF16)
        out.append(piece)
        value = value - piece.astype(F32)
    return out


def extra_rows(heads):
    return -(-2 * PARTS * heads // 16) * 16


def pack_kernel(chunks, head_dim, q_hbm, do_hbm, o_hbm, lse_hbm, k_hbm, v_hbm, *rest):
    count = len(chunks)
    x_refs, kv_refs = rest[:count], rest[count : 2 * count]
    q_ref, do_ref, o_ref, lse_ref, k_ref, v_ref, sems = rest[2 * count :]
    sources = (q_hbm, do_hbm, o_hbm, lse_hbm, k_hbm, v_hbm)
    targets = (q_ref, do_ref, o_ref, lse_ref, k_ref, v_ref)
    copies = [
        pltpu.make_async_copy(source, target, sems.at[i])
        for i, (source, target) in enumerate(zip(sources, targets))
    ]
    for copy in copies:
        copy.start()
    for copy in copies[:4]:
        copy.wait()
    lse = lse_ref[...] * LOG2E
    first = 0
    for heads, out_ref in zip(chunks, x_refs):
        rows = heads * head_dim
        span = slice(first * head_dim, first * head_dim + rows)
        do_t = do_ref[:, span].T
        out_ref[:rows] = q_ref[:, span].T
        out_ref[rows : 2 * rows] = do_t
        product = do_t.astype(F32) * o_ref[:, span].T.astype(F32)
        delta = [
            jnp.sum(product[h * head_dim : (h + 1) * head_dim], axis=0, keepdims=True)
            for h in range(heads)
        ]
        pieces = split_parts(join([lse[first : first + heads]] + delta))
        pad = extra_rows(heads) - 2 * PARTS * heads
        if pad:
            pieces.append(jnp.zeros((pad, lse.shape[1]), BF16))
        out_ref[2 * rows :] = join([piece.astype(F32) for piece in pieces]).astype(BF16)
        first += heads
    for copy in copies[4:]:
        copy.wait()
    first = 0
    for heads, out_ref in zip(chunks, kv_refs):
        rows = heads * head_dim
        span = slice(first * head_dim, first * head_dim + rows)
        out_ref[:rows] = k_ref[:, span].T
        out_ref[rows:] = v_ref[:, span].T
        first += heads


def read_queries(x_ref, heads, head_dim):
    rows = heads * head_dim
    q = [x_ref[h * head_dim : (h + 1) * head_dim] for h in range(heads)]
    do = [x_ref[rows + h * head_dim : rows + (h + 1) * head_dim] for h in range(heads)]
    extra = x_ref[2 * rows :].astype(F32)
    step = 2 * heads
    total = extra[:step]
    for i in range(1, PARTS):
        total = total + extra[i * step : (i + 1) * step]
    lse = [total[h : h + 1] for h in range(heads)]
    delta = [total[heads + h : heads + h + 1] for h in range(heads)]
    return q, do, lse, delta


def read_keys(ref, heads, head_dim):
    rows = heads * head_dim
    k = [ref[h * head_dim : (h + 1) * head_dim] for h in range(heads)]
    v = [ref[rows + h * head_dim : rows + (h + 1) * head_dim] for h in range(heads)]
    return k, v


def task(queries, keys, factor):
    q, do, lse, delta = queries
    k, v = keys
    span = range(len(q))
    scores = [dot(k[i], q[i], TN) for i in span]
    prob_grad = [dot(v[i], do[i], TN) for i in span]
    probs = [jnp.exp2(scores[i] * factor - lse[i]) for i in span]
    score_grad = [(probs[i] * (prob_grad[i] - delta[i])).astype(BF16) for i in span]
    probs = [x.astype(BF16) for x in probs]
    dv = [dot(do[i], probs[i], NT) for i in span]
    dk = [dot(q[i], score_grad[i], NT) for i in span]
    dq = [dot(k[i], score_grad[i], NN) for i in span]
    return dq, dk, dv


def flag_of(keep_ref, count, query, key):
    offset = key - query + RADIUS
    inside = (key >= 0) & (key < count) & (offset >= 0) & (offset < WIN)
    value = keep_ref[query, jnp.clip(offset, 0, WIN - 1)]
    return inside & (value > 0)


def partner_of(place):
    return place + 1 - 2 * lax.rem(place, 2)


def own_kernel(heads, head_dim, factor, count, keep_ref, place_ref, x_ref, cx_ref, kv_ref,
               dq_ref, cdq_ref, dkv_ref):
    place = place_ref[0]
    keys = read_keys(kv_ref, heads, head_dim)
    dq, dk, dv = task(read_queries(x_ref, heads, head_dim), keys, factor)
    dq_ref[...] = join(dq)
    dkv_ref[...] = join(dk + dv)
    flag = flag_of(keep_ref, count, partner_of(place), place)

    @pl.when(flag)
    def _():
        dq, dk, dv = task(
            read_queries(cx_ref, heads, head_dim), read_keys(kv_ref, heads, head_dim), factor
        )
        cdq_ref[...] = join(dq).astype(BF16)
        dkv_ref[...] += join(dk + dv)

    @pl.when(jnp.logical_not(flag))
    def _():
        cdq_ref[...] = jnp.zeros_like(cdq_ref)


def far_kernel(heads, head_dim, factor, count, swapped, first, keep_ref, place_ref, x_ref, kv_ref,
               zkv_ref, *refs):
    if first:
        dq_ref, dkv_ref, zdkv_ref, acc_ref = refs
    else:
        dkv_in, zdkv_in, dq_ref, dkv_ref, zdkv_ref, acc_ref = refs
    place = place_ref[0]
    low = lax.rem(place, 4) < 2
    source = partner_of(place) if swapped else place
    query = jnp.where(low, source + 2, source - 2)
    target = jnp.where(low, place + 4, place - 4)
    flags = [flag_of(keep_ref, count, query, place), flag_of(keep_ref, count, query, target)]
    acc_ref[...] = jnp.zeros_like(acc_ref)
    sides = ((kv_ref, dkv_ref), (zkv_ref, zdkv_ref))
    if not first:
        earlier = (dkv_in, zdkv_in)
    for i, (keys_ref, out_ref) in enumerate(sides):

        @pl.when(flags[i])
        def _(i=i, keys_ref=keys_ref, out_ref=out_ref):
            dq, dk, dv = task(
                read_queries(x_ref, heads, head_dim), read_keys(keys_ref, heads, head_dim), factor
            )
            acc_ref[...] += join(dq)
            total = join(dk + dv)
            if not first:
                total = total + earlier[i][...].astype(F32)
            out_ref[...] = total.astype(out_ref.dtype)

        @pl.when(jnp.logical_not(flags[i]))
        def _(i=i, out_ref=out_ref):
            if first:
                out_ref[...] = jnp.zeros_like(out_ref)
            else:
                out_ref[...] = earlier[i][...].astype(out_ref.dtype)

    dq_ref[...] = acc_ref[...].astype(BF16)


def finish_kernel(chunks, head_dim, scale, *refs):
    ins, outs = refs[:-3], refs[-3:]
    groups = [ins[i * 6 : (i + 1) * 6] for i in range(len(chunks))]
    dq_all, dk_all, dv_all = [], [], []
    for heads, group in zip(chunks, groups):
        dq_own, dq_core, dq_far, dkv_own, dkv_far, zdkv = group
        rows = heads * head_dim
        dq = dq_own[...] + dq_core[...].astype(F32) + dq_far[...].astype(F32)
        total = dkv_own[...] + dkv_far[...] + zdkv[...].astype(F32)
        dq_all.append((dq * scale).astype(BF16))
        dk_all.append((total[:rows] * scale).astype(BF16))
        dv_all.append(total[rows:].astype(BF16))
    for parts, ref in zip((dq_all, dk_all, dv_all), outs):
        ref[...] = join(parts).T


def per_device(query_rows, key_rows, value_rows, out_rows, grad_out, normalizer, keep_tasks):
    tokens, width = query_rows.shape
    head_dim = width // HEADS
    scale = head_dim ** (-0.5)
    factor = scale * LOG2E
    count = lax.axis_size("tok")
    chunks = CHUNK_HEADS
    place = jnp.reshape(lax.axis_index("tok"), (1,)).astype(jnp.int32)

    def send(value, pairs):
        pairs = [(a, b) for a, b in pairs if 0 <= b < count]
        return lax.ppermute(value, "tok", pairs)

    everyone = range(count)
    across = [(i, i ^ 2) for i in everyone]
    core = [(i, i ^ 1) for i in everyone]
    level_in = [(i, i - 4 if i % 4 < 2 else i + 4) for i in everyone]
    level_out = [(i, i + 4 if i % 4 < 2 else i - 4) for i in everyone]

    def shape(rows, dtype):
        return jax.ShapeDtypeStruct((rows, tokens), dtype)

    x_rows = [2 * h * head_dim + extra_rows(h) for h in chunks]
    packed = pl.pallas_call(
        functools.partial(pack_kernel, chunks, head_dim),
        out_shape=[shape(n, BF16) for n in x_rows] + [shape(2 * h * head_dim, BF16) for h in chunks],
        in_specs=[pl.BlockSpec(memory_space=pltpu.HBM)] * 6,
        out_specs=[VMEM] * (2 * len(chunks)),
        scratch_shapes=[pltpu.VMEM((tokens, width), BF16)] * 3
        + [pltpu.VMEM((HEADS, tokens), F32)]
        + [pltpu.VMEM((tokens, width), BF16)] * 2
        + [pltpu.SemaphoreType.DMA((6,))],
        compiler_params=params(),
        name="pack",
    )(query_rows, grad_out, out_rows, normalizer, key_rows, value_rows)
    x_own, kv_own = packed[: len(chunks)], packed[len(chunks) :]
    x_far = [send(x, across) for x in x_own]
    kv_level = [send(kv, level_in) for kv in kv_own]
    x_core = [send(x, core) for x in x_own]
    x_far_core = [send(x, core) for x in x_far]

    finish_args = []
    for c, heads in enumerate(chunks):
        rows = heads * head_dim
        work = 10 * tokens * tokens * 256 * heads

        def far(swapped, first, x, *earlier):
            return pl.pallas_call(
                functools.partial(far_kernel, heads, head_dim, factor, count, swapped, first),
                out_shape=[shape(rows, BF16), shape(2 * rows, F32), shape(2 * rows, F32 if first else BF16)],
                in_specs=[SMEM] * 2 + [VMEM] * (3 + len(earlier)),
                out_specs=[VMEM] * 3,
                scratch_shapes=[pltpu.VMEM((rows, tokens), F32)],
                compiler_params=params(),
                cost_estimate=cost(2 * work, 16 * rows * tokens * 2),
                name="far_tasks",
            )(keep_tasks, place, x, kv_own[c], kv_level[c], *earlier)

        dq_own, dq_core, dkv_own = pl.pallas_call(
            functools.partial(own_kernel, heads, head_dim, factor, count),
            out_shape=[shape(rows, F32), shape(rows, BF16), shape(2 * rows, F32)],
            in_specs=[SMEM] * 2 + [VMEM] * 3,
            out_specs=[VMEM] * 3,
            compiler_params=params(),
            cost_estimate=cost(2 * work, 8 * rows * tokens * 2),
            name="own_tasks",
        )(keep_tasks, place, x_own[c], x_core[c], kv_own[c])
        dq_a, dkv_a, zdkv_a = far(False, True, x_far[c])
        dq_b, dkv_far, zdkv = far(True, False, x_far_core[c], dkv_a, zdkv_a)
        dq_far = (dq_a.astype(F32) + send(dq_b, core).astype(F32)).astype(BF16)
        finish_args += [
            dq_own,
            send(dq_core, core),
            send(dq_far, across),
            dkv_own,
            dkv_far,
            send(zdkv, level_out),
        ]
    grad_query, grad_key, grad_value = pl.pallas_call(
        functools.partial(finish_kernel, chunks, head_dim, scale),
        out_shape=[jax.ShapeDtypeStruct((tokens, width), BF16)] * 3,
        in_specs=[VMEM] * len(finish_args),
        out_specs=[VMEM] * 3,
        compiler_params=params(),
        name="finish",
    )(*finish_args)
    return grad_query, grad_key, grad_value


def solution(mesh):
    rows = P(("groups", "tok"), None)
    return jax.shard_map(
        per_device,
        mesh=mesh,
        in_specs=(rows, rows, rows, rows, rows, P(None, ("groups", "tok")), P("groups", None)),
        out_specs=(rows, rows, rows),
        check_vma=False,
    )
```

```python
import functools
import math

import jax
import jax.numpy as jnp
from jax import lax
from jax.experimental import pallas as pl
from jax.experimental.pallas import tpu as pltpu
from jax.sharding import PartitionSpec as P

HEADS = 16
RADIUS = 2
WIN = 5
PARTS = 3
CHUNK_HEADS = (8, 8)
PACK_MIB = 60
NN = (((1,), (0,)), ((), ()))
NT = (((1,), (1,)), ((), ()))
TN = (((0,), (0,)), ((), ()))
LOG2E = math.log2(math.e)
F32 = jnp.float32
BF16 = jnp.bfloat16
VMEM = pl.BlockSpec(memory_space=pltpu.VMEM)
SMEM = pl.BlockSpec(memory_space=pltpu.SMEM)


def dot(left, right, dims):
    return lax.dot_general(left, right, dims, preferred_element_type=F32)


def join(parts):
    return jnp.concatenate(parts, axis=0)


def params(mib=40):
    return pltpu.CompilerParams(vmem_limit_bytes=mib * 1024 * 1024)


def after(value, *tokens):
    return lax.optimization_barrier((value,) + tokens)[0]


def cost(flops, size):
    return pl.CostEstimate(flops=flops, bytes_accessed=size, transcendentals=0)


def split_parts(value):
    out = []
    for _ in range(PARTS):
        piece = value.astype(BF16)
        out.append(piece)
        value = value - piece.astype(F32)
    return out


def extra_rows(heads):
    return -(-2 * PARTS * heads // 16) * 16


def pack_kernel(chunks, head_dim, q_hbm, do_hbm, o_hbm, lse_hbm, k_hbm, v_hbm, *rest):
    count = len(chunks)
    x_refs, kv_refs = rest[:count], rest[count : 2 * count]
    q_ref, do_ref, o_ref, lse_ref, k_ref, v_ref, sems = rest[2 * count :]
    sources = (q_hbm, do_hbm, o_hbm, lse_hbm, k_hbm, v_hbm)
    targets = (q_ref, do_ref, o_ref, lse_ref, k_ref, v_ref)
    copies = [
        pltpu.make_async_copy(source, target, sems.at[i])
        for i, (source, target) in enumerate(zip(sources, targets))
    ]
    for copy in copies:
        copy.start()
    for copy in copies[:4]:
        copy.wait()
    lse = lse_ref[...] * LOG2E
    first = 0
    for heads, out_ref in zip(chunks, x_refs):
        rows = heads * head_dim
        span = slice(first * head_dim, first * head_dim + rows)
        do_t = do_ref[:, span].T
        out_ref[:rows] = q_ref[:, span].T
        out_ref[rows : 2 * rows] = do_t
        product = do_t.astype(F32) * o_ref[:, span].T.astype(F32)
        delta = [
            jnp.sum(product[h * head_dim : (h + 1) * head_dim], axis=0, keepdims=True)
            for h in range(heads)
        ]
        pieces = split_parts(join([lse[first : first + heads]] + delta))
        pad = extra_rows(heads) - 2 * PARTS * heads
        if pad:
            pieces.append(jnp.zeros((pad, lse.shape[1]), BF16))
        out_ref[2 * rows :] = join([piece.astype(F32) for piece in pieces]).astype(BF16)
        first += heads
    for copy in copies[4:]:
        copy.wait()
    first = 0
    for heads, out_ref in zip(chunks, kv_refs):
        rows = heads * head_dim
        span = slice(first * head_dim, first * head_dim + rows)
        out_ref[:rows] = k_ref[:, span].T
        out_ref[rows:] = v_ref[:, span].T
        first += heads


def read_queries(x_ref, heads, head_dim):
    rows = heads * head_dim
    q = [x_ref[h * head_dim : (h + 1) * head_dim] for h in range(heads)]
    do = [x_ref[rows + h * head_dim : rows + (h + 1) * head_dim] for h in range(heads)]
    extra = x_ref[2 * rows :].astype(F32)
    step = 2 * heads
    total = extra[:step]
    for i in range(1, PARTS):
        total = total + extra[i * step : (i + 1) * step]
    lse = [total[h : h + 1] for h in range(heads)]
    delta = [total[heads + h : heads + h + 1] for h in range(heads)]
    return q, do, lse, delta


def read_keys(ref, heads, head_dim):
    rows = heads * head_dim
    k = [ref[h * head_dim : (h + 1) * head_dim] for h in range(heads)]
    v = [ref[rows + h * head_dim : rows + (h + 1) * head_dim] for h in range(heads)]
    return k, v


def task(queries, keys, factor):
    q, do, lse, delta = queries
    k, v = keys
    span = range(len(q))
    scores = [dot(k[i], q[i], TN) for i in span]
    prob_grad = [dot(v[i], do[i], TN) for i in span]
    probs = [jnp.exp2(scores[i] * factor - lse[i]) for i in span]
    score_grad = [(probs[i] * (prob_grad[i] - delta[i])).astype(BF16) for i in span]
    probs = [x.astype(BF16) for x in probs]
    dv = [dot(do[i], probs[i], NT) for i in span]
    dk = [dot(q[i], score_grad[i], NT) for i in span]
    dq = [dot(k[i], score_grad[i], NN) for i in span]
    return dq, dk, dv


def flag_of(keep_ref, count, query, key):
    offset = key - query + RADIUS
    inside = (key >= 0) & (key < count) & (offset >= 0) & (offset < WIN)
    value = keep_ref[query, jnp.clip(offset, 0, WIN - 1)]
    return inside & (value > 0)


def partner_of(place):
    return place + 1 - 2 * lax.rem(place, 2)


def own_kernel(heads, head_dim, factor, count, keep_ref, place_ref, x_ref, cx_ref, kv_ref,
               dq_ref, cdq_ref, dkv_ref):
    place = place_ref[0]
    keys = read_keys(kv_ref, heads, head_dim)
    dq, dk, dv = task(read_queries(x_ref, heads, head_dim), keys, factor)
    dq_ref[...] = join(dq)
    dkv_ref[...] = join(dk + dv)
    flag = flag_of(keep_ref, count, partner_of(place), place)

    @pl.when(flag)
    def _():
        dq, dk, dv = task(
            read_queries(cx_ref, heads, head_dim), read_keys(kv_ref, heads, head_dim), factor
        )
        cdq_ref[...] = join(dq).astype(BF16)
        dkv_ref[...] += join(dk + dv)

    @pl.when(jnp.logical_not(flag))
    def _():
        cdq_ref[...] = jnp.zeros_like(cdq_ref)


def far_kernel(heads, head_dim, factor, count, swapped, first, keep_ref, place_ref, x_ref, kv_ref,
               zkv_ref, *refs):
    if first:
        dq_ref, dkv_ref, zdkv_ref, acc_ref = refs
    else:
        dkv_in, zdkv_in, dq_ref, dkv_ref, zdkv_ref, acc_ref = refs
    place = place_ref[0]
    low = lax.rem(place, 4) < 2
    source = partner_of(place) if swapped else place
    query = jnp.where(low, source + 2, source - 2)
    target = jnp.where(low, place + 4, place - 4)
    flags = [flag_of(keep_ref, count, query, place), flag_of(keep_ref, count, query, target)]
    acc_ref[...] = jnp.zeros_like(acc_ref)
    sides = ((kv_ref, dkv_ref), (zkv_ref, zdkv_ref))
    if not first:
        earlier = (dkv_in, zdkv_in)
    for i, (keys_ref, out_ref) in enumerate(sides):

        @pl.when(flags[i])
        def _(i=i, keys_ref=keys_ref, out_ref=out_ref):
            dq, dk, dv = task(
                read_queries(x_ref, heads, head_dim), read_keys(keys_ref, heads, head_dim), factor
            )
            acc_ref[...] += join(dq)
            total = join(dk + dv)
            if not first:
                total = total + earlier[i][...].astype(F32)
            out_ref[...] = total.astype(out_ref.dtype)

        @pl.when(jnp.logical_not(flags[i]))
        def _(i=i, out_ref=out_ref):
            if first:
                out_ref[...] = jnp.zeros_like(out_ref)
            else:
                out_ref[...] = earlier[i][...].astype(out_ref.dtype)

    dq_ref[...] = acc_ref[...].astype(BF16)


def finish_kernel(chunks, head_dim, scale, *refs):
    ins, outs = refs[:-3], refs[-3:]
    groups = [ins[i * 6 : (i + 1) * 6] for i in range(len(chunks))]
    dq_all, dk_all, dv_all = [], [], []
    for heads, group in zip(chunks, groups):
        dq_own, dq_core, dq_far, dkv_own, dkv_far, zdkv = group
        rows = heads * head_dim
        dq = dq_own[...] + dq_core[...].astype(F32) + dq_far[...].astype(F32)
        total = dkv_own[...] + dkv_far[...] + zdkv[...].astype(F32)
        dq_all.append((dq * scale).astype(BF16))
        dk_all.append((total[:rows] * scale).astype(BF16))
        dv_all.append(total[rows:].astype(BF16))
    for parts, ref in zip((dq_all, dk_all, dv_all), outs):
        ref[...] = join(parts).T


def per_device(query_rows, key_rows, value_rows, out_rows, grad_out, normalizer, keep_tasks):
    tokens, width = query_rows.shape
    head_dim = width // HEADS
    scale = head_dim ** (-0.5)
    factor = scale * LOG2E
    count = lax.axis_size("tok")
    chunks = CHUNK_HEADS
    place = jnp.reshape(lax.axis_index("tok"), (1,)).astype(jnp.int32)

    def send(value, pairs):
        pairs = [(a, b) for a, b in pairs if 0 <= b < count]
        return lax.ppermute(value, "tok", pairs)

    everyone = range(count)
    across = [(i, i ^ 2) for i in everyone]
    core = [(i, i ^ 1) for i in everyone]
    level_in = [(i, i - 4 if i % 4 < 2 else i + 4) for i in everyone]
    level_out = [(i, i + 4 if i % 4 < 2 else i - 4) for i in everyone]

    def shape(rows, dtype):
        return jax.ShapeDtypeStruct((rows, tokens), dtype)

    x_rows = [2 * h * head_dim + extra_rows(h) for h in chunks]
    packed = pl.pallas_call(
        functools.partial(pack_kernel, chunks, head_dim),
        out_shape=[shape(n, BF16) for n in x_rows] + [shape(2 * h * head_dim, BF16) for h in chunks],
        in_specs=[pl.BlockSpec(memory_space=pltpu.HBM)] * 6,
        out_specs=[VMEM] * (2 * len(chunks)),
        scratch_shapes=[pltpu.VMEM((tokens, width), BF16)] * 3
        + [pltpu.VMEM((HEADS, tokens), F32)]
        + [pltpu.VMEM((tokens, width), BF16)] * 2
        + [pltpu.SemaphoreType.DMA((6,))],
        compiler_params=params(PACK_MIB),
        name="pack",
    )(query_rows, grad_out, out_rows, normalizer, key_rows, value_rows)
    x_own, kv_own = packed[: len(chunks)], packed[len(chunks) :]
    x_far = [send(x, across) for x in x_own]
    kv_level = [send(kv, level_in) for kv in kv_own]
    x_core = [send(x, core) for x in x_own]

    own, mine, finish_args, done = [], [], [], None
    for c, heads in enumerate(chunks):
        rows = heads * head_dim
        work = 10 * tokens * tokens * 256 * heads

        def far(swapped, first, x, *earlier):
            return pl.pallas_call(
                functools.partial(far_kernel, heads, head_dim, factor, count, swapped, first),
                out_shape=[shape(rows, BF16), shape(2 * rows, F32), shape(2 * rows, F32 if first else BF16)],
                in_specs=[SMEM] * 2 + [VMEM] * (3 + len(earlier)),
                out_specs=[VMEM] * 3,
                scratch_shapes=[pltpu.VMEM((rows, tokens), F32)],
                compiler_params=params(),
                cost_estimate=cost(2 * work, 16 * rows * tokens * 2),
                name="far_tasks",
            )(keep_tasks, place, x, kv_own[c], kv_level[c], *earlier)

        def own_tasks(x, x_c, kv, c=c, heads=heads, rows=rows, work=work):
            return pl.pallas_call(
                functools.partial(own_kernel, heads, head_dim, factor, count),
                out_shape=[shape(rows, F32), shape(rows, BF16), shape(2 * rows, F32)],
                in_specs=[SMEM] * 2 + [VMEM] * 3,
                out_specs=[VMEM] * 3,
                compiler_params=params(),
                cost_estimate=cost(2 * work, 8 * rows * tokens * 2),
                name="own_tasks",
            )(keep_tasks, place, x, x_c, kv)

        own.append(own_tasks)
        x = x_far[c]
        if c:
            x = after(x, done)
        else:
            mine.append(own_tasks(x_own[c], x_core[c], kv_own[c]))
            x = after(x, mine[0][0])
        dq_a, dkv_a, zdkv_a = far(False, True, x)
        dq_b, dkv_far, zdkv = far(True, False, send(x, core), dkv_a, zdkv_a)
        dq_far = (dq_a.astype(F32) + send(dq_b, core).astype(F32)).astype(BF16)
        done = dq_b
        finish_args.append((send(dq_far, across), dkv_far, send(zdkv, level_out)))
    for c in range(1, len(chunks)):
        mine.append(own[c](after(x_own[c], done), x_core[c], kv_own[c]))
    finish_args = [
        value
        for (dq_own, dq_core, dkv_own), (dq_far, dkv_far, zdkv) in zip(mine, finish_args)
        for value in (dq_own, send(dq_core, core), dq_far, dkv_own, dkv_far, zdkv)
    ]
    grad_query, grad_key, grad_value = pl.pallas_call(
        functools.partial(finish_kernel, chunks, head_dim, scale),
        out_shape=[jax.ShapeDtypeStruct((tokens, width), BF16)] * 3,
        in_specs=[VMEM] * len(finish_args),
        out_specs=[VMEM] * 3,
        compiler_params=params(),
        name="finish",
    )(*finish_args)
    return grad_query, grad_key, grad_value


def solution(mesh):
    rows = P(("groups", "tok"), None)
    return jax.shard_map(
        per_device,
        mesh=mesh,
        in_specs=(rows, rows, rows, rows, rows, P(None, ("groups", "tok")), P("groups", None)),
        out_specs=(rows, rows, rows),
        check_vma=False,
    )
```

```python
import functools
import math

import jax
import jax.numpy as jnp
from jax import lax
from jax.experimental import pallas as pl
from jax.experimental.pallas import tpu as pltpu
from jax.sharding import PartitionSpec as P

HEADS = 16
RADIUS = 2
WIN = 5
PARTS = 3
CHUNK_HEADS = (8, 8)
HOPS = 2
CORE_COST, FAR_COST, SELF_COST = (0.01, 0.01, 0.01)
NN = (((1,), (0,)), ((), ()))
NT = (((1,), (1,)), ((), ()))
TN = (((0,), (0,)), ((), ()))
LOG2E = math.log2(math.e)
F32 = jnp.float32
BF16 = jnp.bfloat16
VMEM = pl.BlockSpec(memory_space=pltpu.VMEM)
SMEM = pl.BlockSpec(memory_space=pltpu.SMEM)


def dot(left, right, dims):
    return lax.dot_general(left, right, dims, preferred_element_type=F32)


def join(parts):
    return jnp.concatenate(parts, axis=0)


def params(mib=40):
    return pltpu.CompilerParams(vmem_limit_bytes=mib * 1024 * 1024)


def after(value, *tokens):
    return lax.optimization_barrier((value,) + tokens)[0]


def cost(flops, size):
    return pl.CostEstimate(flops=flops, bytes_accessed=size, transcendentals=0)


def split_parts(value):
    out = []
    for _ in range(PARTS):
        piece = value.astype(BF16)
        out.append(piece)
        value = value - piece.astype(F32)
    return out


def extra_rows(heads):
    return -(-2 * PARTS * heads // 16) * 16


def pack_kernel(chunks, head_dim, q_hbm, do_hbm, o_hbm, lse_hbm, k_hbm, v_hbm, *rest):
    count = len(chunks)
    x_refs, kv_refs = rest[:count], rest[count : 2 * count]
    q_ref, do_ref, o_ref, lse_ref, k_ref, v_ref, sems = rest[2 * count :]
    sources = (q_hbm, do_hbm, o_hbm, lse_hbm, k_hbm, v_hbm)
    targets = (q_ref, do_ref, o_ref, lse_ref, k_ref, v_ref)
    copies = [
        pltpu.make_async_copy(source, target, sems.at[i])
        for i, (source, target) in enumerate(zip(sources, targets))
    ]
    for copy in copies:
        copy.start()
    for copy in copies[:4]:
        copy.wait()
    lse = lse_ref[...] * LOG2E
    first = 0
    for heads, out_ref in zip(chunks, x_refs):
        rows = heads * head_dim
        span = slice(first * head_dim, first * head_dim + rows)
        do_t = do_ref[:, span].T
        out_ref[:rows] = q_ref[:, span].T
        out_ref[rows : 2 * rows] = do_t
        product = do_t.astype(F32) * o_ref[:, span].T.astype(F32)
        delta = [
            jnp.sum(product[h * head_dim : (h + 1) * head_dim], axis=0, keepdims=True)
            for h in range(heads)
        ]
        pieces = split_parts(join([lse[first : first + heads]] + delta))
        pad = extra_rows(heads) - 2 * PARTS * heads
        if pad:
            pieces.append(jnp.zeros((pad, lse.shape[1]), BF16))
        out_ref[2 * rows :] = join([piece.astype(F32) for piece in pieces]).astype(BF16)
        first += heads
    for copy in copies[4:]:
        copy.wait()
    first = 0
    for heads, out_ref in zip(chunks, kv_refs):
        rows = heads * head_dim
        span = slice(first * head_dim, first * head_dim + rows)
        out_ref[:rows] = k_ref[:, span].T
        out_ref[rows:] = v_ref[:, span].T
        first += heads


def read_queries(x_refs, heads, head_dim):
    blocks = []
    for ref in x_refs:
        blocks += [ref[i : i + head_dim] for i in range(0, 2 * heads * head_dim, head_dim) if i < ref.shape[0]]
    q, do = blocks[:heads], blocks[heads : 2 * heads]
    extra = x_refs[-1][-extra_rows(heads) :].astype(F32)
    step = 2 * heads
    total = extra[:step]
    for i in range(1, PARTS):
        total = total + extra[i * step : (i + 1) * step]
    lse = [total[h : h + 1] for h in range(heads)]
    delta = [total[heads + h : heads + h + 1] for h in range(heads)]
    return q, do, lse, delta


def read_keys(ref, heads, head_dim):
    rows = heads * head_dim
    k = [ref[h * head_dim : (h + 1) * head_dim] for h in range(heads)]
    v = [ref[rows + h * head_dim : rows + (h + 1) * head_dim] for h in range(heads)]
    return k, v


def task(queries, keys, factor):
    q, do, lse, delta = queries
    k, v = keys
    span = range(len(q))
    scores = [dot(k[i], q[i], TN) for i in span]
    prob_grad = [dot(v[i], do[i], TN) for i in span]
    probs = [jnp.exp2(scores[i] * factor - lse[i]) for i in span]
    score_grad = [(probs[i] * (prob_grad[i] - delta[i])).astype(BF16) for i in span]
    probs = [x.astype(BF16) for x in probs]
    dv = [dot(do[i], probs[i], NT) for i in span]
    dk = [dot(q[i], score_grad[i], NT) for i in span]
    dq = [dot(k[i], score_grad[i], NN) for i in span]
    return dq, dk, dv


def flag_of(keep_ref, count, query, key):
    offset = key - query + RADIUS
    inside = (key >= 0) & (key < count) & (offset >= 0) & (offset < WIN)
    value = keep_ref[query, jnp.clip(offset, 0, WIN - 1)]
    return inside & (value > 0)


def partner_of(place):
    return place + 1 - 2 * lax.rem(place, 2)


def near_kernel(chunks, head_dim, factor, count, swapped, keep_ref, place_ref, *refs):
    size = len(chunks)
    x_refs, kv_refs = refs[:size], refs[size : 2 * size]
    outs = refs[2 * size :]
    place = place_ref[0]
    flag = flag_of(keep_ref, count, partner_of(place) if swapped else place, place)
    for c, heads in enumerate(chunks):
        dq_ref, dkv_ref = outs[2 * c : 2 * c + 2]

        @pl.when(flag)
        def _(c=c, heads=heads, dq_ref=dq_ref, dkv_ref=dkv_ref):
            dq, dk, dv = task(
                read_queries(x_refs[c : c + 1], heads, head_dim), read_keys(kv_refs[c], heads, head_dim), factor
            )
            dq_ref[...] = join(dq).astype(dq_ref.dtype)
            dkv_ref[...] = join(dk + dv)

        @pl.when(jnp.logical_not(flag))
        def _(dq_ref=dq_ref, dkv_ref=dkv_ref):
            dq_ref[...] = jnp.zeros_like(dq_ref)
            dkv_ref[...] = jnp.zeros_like(dkv_ref)


def far_kernel(heads, head_dim, factor, count, level, first, keep_ref, place_ref, x_ref, *refs):
    c_refs, kv_ref, refs = refs[:HOPS], refs[HOPS], refs[HOPS + 1 :]
    if first:
        earlier, (dq_ref, cdq_ref, dkv_ref, acc_ref) = None, refs
    else:
        earlier, (dq_ref, cdq_ref, dkv_ref, acc_ref) = refs[:2], refs[2:]
    place = place_ref[0]
    jump = jnp.where(lax.rem(place, 4) < 2, 2, -2)
    target = place + 2 * jump if level else place
    acc_ref[...] = jnp.zeros_like(acc_ref)
    slots = ((place + jump, (x_ref,), dq_ref), (partner_of(place) + jump, c_refs, cdq_ref))
    for i, (query, queries_ref, out_ref) in enumerate(slots):
        flag = flag_of(keep_ref, count, query, target)

        @pl.when(flag)
        def _(i=i, queries_ref=queries_ref, out_ref=out_ref):
            dq, dk, dv = task(
                read_queries(queries_ref, heads, head_dim), read_keys(kv_ref, heads, head_dim), factor
            )
            total = join(dq) if first else earlier[i][...] + join(dq)
            out_ref[...] = total.astype(out_ref.dtype)
            acc_ref[...] += join(dk + dv)

        @pl.when(jnp.logical_not(flag))
        def _(i=i, out_ref=out_ref):
            if first:
                out_ref[...] = jnp.zeros_like(out_ref)
            else:
                out_ref[...] = earlier[i][...].astype(out_ref.dtype)

    dkv_ref[...] = acc_ref[...].astype(dkv_ref.dtype)


def finish_kernel(chunks, head_dim, scale, *refs):
    ins, outs = refs[:-3], refs[-3:]
    groups = [ins[i * 7 : (i + 1) * 7] for i in range(len(chunks))]
    dq_all, dk_all, dv_all = [], [], []
    for heads, group in zip(chunks, groups):
        dq_own, dq_core, dq_far, dkv_own, dkv_core, dkv_far, zdkv = group
        rows = heads * head_dim
        dq = dq_own[...] + dq_core[...].astype(F32) + dq_far[...].astype(F32)
        total = dkv_own[...] + dkv_core[...] + dkv_far[...] + zdkv[...].astype(F32)
        dq_all.append((dq * scale).astype(BF16))
        dk_all.append((total[:rows] * scale).astype(BF16))
        dv_all.append(total[rows:].astype(BF16))
    for parts, ref in zip((dq_all, dk_all, dv_all), outs):
        ref[...] = join(parts).T


def per_device(query_rows, key_rows, value_rows, out_rows, grad_out, normalizer, keep_tasks):
    tokens, width = query_rows.shape
    head_dim = width // HEADS
    scale = head_dim ** (-0.5)
    factor = scale * LOG2E
    count = lax.axis_size("tok")
    chunks = CHUNK_HEADS
    place = jnp.reshape(lax.axis_index("tok"), (1,)).astype(jnp.int32)

    def send(value, pairs):
        return lax.ppermute(value, "tok", [(a, b % count) for a, b in pairs])

    everyone = range(count)
    across = [(i, i ^ 2) for i in everyone]
    core = [(i, i ^ 1) for i in everyone]
    level_in = [(i, i - 4 if i % 4 < 2 else i + 4) for i in everyone]
    level_out = [(i, i + 4 if i % 4 < 2 else i - 4) for i in everyone]

    def shape(rows, dtype):
        return jax.ShapeDtypeStruct((rows, tokens), dtype)

    x_rows = [2 * h * head_dim + extra_rows(h) for h in chunks]
    packed = pl.pallas_call(
        functools.partial(pack_kernel, chunks, head_dim),
        out_shape=[shape(n, BF16) for n in x_rows] + [shape(2 * h * head_dim, BF16) for h in chunks],
        in_specs=[pl.BlockSpec(memory_space=pltpu.HBM)] * 6,
        out_specs=[VMEM] * (2 * len(chunks)),
        scratch_shapes=[pltpu.VMEM((tokens, width), BF16)] * 3
        + [pltpu.VMEM((HEADS, tokens), F32)]
        + [pltpu.VMEM((tokens, width), BF16)] * 2
        + [pltpu.SemaphoreType.DMA((6,))],
        compiler_params=params(),
        name="pack",
    )(
        *[
            pltpu.with_memory_space_constraint(value, pltpu.HBM)
            for value in (query_rows, grad_out, out_rows, normalizer, key_rows, value_rows)
        ]
    )
    x_own, kv_own = packed[: len(chunks)], packed[len(chunks) :]
    x_far = [send(x, across) for x in x_own]
    kv_level = [send(kv, level_in) for kv in kv_own]
    x_core = [send(x, core) for x in x_own]

    def work_of(heads):
        return 10 * tokens * tokens * 256 * heads

    def near(swapped, xs, dq_type, share):
        out = []
        for heads in chunks:
            rows = heads * head_dim
            out += [shape(rows, dq_type), shape(2 * rows, F32)]
        got = pl.pallas_call(
            functools.partial(near_kernel, chunks, head_dim, factor, count, swapped),
            out_shape=out,
            in_specs=[SMEM] * 2 + [VMEM] * (2 * len(chunks)),
            out_specs=[VMEM] * len(out),
            compiler_params=params(),
            cost_estimate=cost(int(work_of(HEADS) * share), 1024),
            name="near_tasks",
        )(keep_tasks, place, *xs, *kv_own)
        return got[::2], got[1::2]

    def far(c, level, x, hop, keys, earlier):
        rows = chunks[c] * head_dim
        dq_type = BF16 if earlier else F32
        return pl.pallas_call(
            functools.partial(far_kernel, chunks[c], head_dim, factor, count, level, not earlier),
            out_shape=[shape(rows, dq_type)] * 2 + [shape(2 * rows, BF16 if level else F32)],
            in_specs=[SMEM] * 2 + [VMEM] * (2 + HOPS + len(earlier)),
            out_specs=[VMEM] * 3,
            scratch_shapes=[pltpu.VMEM((2 * rows, tokens), F32)],
            compiler_params=params(),
            cost_estimate=cost(int(work_of(chunks[c]) * FAR_COST), 1024),
            name="far_tasks",
        )(keep_tasks, place, x, *hop, keys, *earlier)

    done = x_core[0]
    far_out = []
    for c in range(len(chunks)):
        x = after(x_far[c], done)
        cuts = [2 * chunks[c] * i // HOPS * head_dim for i in range(HOPS)] + [x.shape[0]]
        cuts = [-(-cut // head_dim) * head_dim for cut in cuts]
        hop = [send(x[i:j], core) for i, j in zip(cuts, cuts[1:])]
        dq_x, dq_c, dkv_far = far(c, False, x, hop, kv_own[c], ())
        z = after(kv_level[c], dq_x)
        dq_x, dq_c, zdkv = far(c, True, x, hop, z, (dq_x, dq_c))
        done = dq_x
        dq_far = (dq_x.astype(F32) + send(dq_c, core).astype(F32)).astype(BF16)
        far_out.append((send(dq_far, across), dkv_far, send(zdkv, level_out)))
    dq_core, dkv_core = near(True, [after(value, done) for value in x_core], BF16, CORE_COST)
    done = dq_core[0]
    dq_own, dkv_own = near(False, [after(x, done, far_out[0][2]) for x in x_own], F32, SELF_COST)
    finish_args = []
    for c in range(len(chunks)):
        dq_far, dkv_far, zdkv = far_out[c]
        finish_args += [
            dq_own[c],
            send(dq_core[c], core),
            dq_far,
            dkv_own[c],
            dkv_core[c],
            dkv_far,
            zdkv,
        ]
    grad_query, grad_key, grad_value = pl.pallas_call(
        functools.partial(finish_kernel, chunks, head_dim, scale),
        out_shape=[jax.ShapeDtypeStruct((tokens, width), BF16)] * 3,
        in_specs=[VMEM] * len(finish_args),
        out_specs=[VMEM] * 3,
        compiler_params=params(),
        name="finish",
    )(*finish_args)
    return grad_query, grad_key, grad_value


def solution(mesh):
    rows = P(("groups", "tok"), None)
    return jax.shard_map(
        per_device,
        mesh=mesh,
        in_specs=(rows, rows, rows, rows, rows, P(None, ("groups", "tok")), P("groups", None)),
        out_specs=(rows, rows, rows),
        check_vma=False,
    )
```

```python
import functools
import math

import jax
import jax.numpy as jnp
from jax import lax
from jax.experimental import pallas as pl
from jax.experimental.pallas import tpu as pltpu
from jax.sharding import PartitionSpec as P

HEADS = 16
RADIUS = 2
WIN = 5
PARTS = 3
CHUNK_HEADS = (8, 8)
HOPS = 2
CORE_COST, FAR_COST, SELF_COST = (0.01, 0.01, 0.01)
NN = (((1,), (0,)), ((), ()))
NT = (((1,), (1,)), ((), ()))
TN = (((0,), (0,)), ((), ()))
LOG2E = math.log2(math.e)
F32 = jnp.float32
BF16 = jnp.bfloat16
VMEM = pl.BlockSpec(memory_space=pltpu.VMEM)
SMEM = pl.BlockSpec(memory_space=pltpu.SMEM)


def dot(left, right, dims):
    return lax.dot_general(left, right, dims, preferred_element_type=F32)


def join(parts):
    return jnp.concatenate(parts, axis=0)


def params(mib=24):
    return pltpu.CompilerParams(vmem_limit_bytes=mib * 1024 * 1024)


def after(value, *tokens):
    return lax.optimization_barrier((value,) + tokens)[0]


def cost(flops, size):
    return pl.CostEstimate(flops=flops, bytes_accessed=size, transcendentals=0)


def split_parts(value):
    out = []
    for _ in range(PARTS):
        piece = value.astype(BF16)
        out.append(piece)
        value = value - piece.astype(F32)
    return out


def extra_rows(heads):
    return -(-2 * PARTS * heads // 16) * 16


def fetch(sources, targets, sems):
    copies = [
        pltpu.make_async_copy(source, target, sems.at[i])
        for i, (source, target) in enumerate(zip(sources, targets))
    ]
    for copy in copies:
        copy.start()
    for copy in copies:
        copy.wait()


def pack_queries(chunks, head_dim, q_hbm, do_hbm, o_hbm, lse_hbm, *rest):
    x_refs, (q_ref, do_ref, o_ref, lse_ref, sems) = rest[: len(chunks)], rest[len(chunks) :]
    fetch((q_hbm, do_hbm, o_hbm, lse_hbm), (q_ref, do_ref, o_ref, lse_ref), sems)
    lse = lse_ref[...] * LOG2E
    first = 0
    for heads, out_ref in zip(chunks, x_refs):
        rows = heads * head_dim
        span = slice(first * head_dim, first * head_dim + rows)
        do_t = do_ref[:, span].T
        out_ref[:rows] = q_ref[:, span].T
        out_ref[rows : 2 * rows] = do_t
        product = do_t.astype(F32) * o_ref[:, span].T.astype(F32)
        delta = [
            jnp.sum(product[h * head_dim : (h + 1) * head_dim], axis=0, keepdims=True)
            for h in range(heads)
        ]
        pieces = split_parts(join([lse[first : first + heads]] + delta))
        pad = extra_rows(heads) - 2 * PARTS * heads
        if pad:
            pieces.append(jnp.zeros((pad, lse.shape[1]), BF16))
        out_ref[2 * rows :] = join([piece.astype(F32) for piece in pieces]).astype(BF16)
        first += heads


def pack_keys(chunks, head_dim, k_hbm, v_hbm, token_ref, *rest):
    kv_refs, (k_ref, v_ref, sems) = rest[: len(chunks)], rest[len(chunks) :]
    fetch((k_hbm, v_hbm), (k_ref, v_ref), sems)
    first = 0
    for heads, out_ref in zip(chunks, kv_refs):
        rows = heads * head_dim
        span = slice(first * head_dim, first * head_dim + rows)
        out_ref[:rows] = k_ref[:, span].T
        out_ref[rows:] = v_ref[:, span].T
        first += heads


def read_queries(x_refs, heads, head_dim):
    blocks = []
    for ref in x_refs:
        blocks += [ref[i : i + head_dim] for i in range(0, 2 * heads * head_dim, head_dim) if i < ref.shape[0]]
    q, do = blocks[:heads], blocks[heads : 2 * heads]
    extra = x_refs[-1][-extra_rows(heads) :].astype(F32)
    step = 2 * heads
    total = extra[:step]
    for i in range(1, PARTS):
        total = total + extra[i * step : (i + 1) * step]
    lse = [total[h : h + 1] for h in range(heads)]
    delta = [total[heads + h : heads + h + 1] for h in range(heads)]
    return q, do, lse, delta


def read_keys(ref, heads, head_dim):
    rows = heads * head_dim
    k = [ref[h * head_dim : (h + 1) * head_dim] for h in range(heads)]
    v = [ref[rows + h * head_dim : rows + (h + 1) * head_dim] for h in range(heads)]
    return k, v


def task(queries, keys, factor):
    q, do, lse, delta = queries
    k, v = keys
    span = range(len(q))
    scores = [dot(k[i], q[i], TN) for i in span]
    prob_grad = [dot(v[i], do[i], TN) for i in span]
    probs = [jnp.exp2(scores[i] * factor - lse[i]) for i in span]
    score_grad = [(probs[i] * (prob_grad[i] - delta[i])).astype(BF16) for i in span]
    probs = [x.astype(BF16) for x in probs]
    dv = [dot(do[i], probs[i], NT) for i in span]
    dk = [dot(q[i], score_grad[i], NT) for i in span]
    dq = [dot(k[i], score_grad[i], NN) for i in span]
    return dq, dk, dv


def flag_of(keep_ref, count, query, key):
    offset = key - query + RADIUS
    inside = (key >= 0) & (key < count) & (offset >= 0) & (offset < WIN)
    value = keep_ref[query, jnp.clip(offset, 0, WIN - 1)]
    return inside & (value > 0)


def partner_of(place):
    return place + 1 - 2 * lax.rem(place, 2)


def near_kernel(chunks, head_dim, factor, count, swapped, keep_ref, place_ref, *refs):
    size = len(chunks)
    x_refs, kv_refs = refs[:size], refs[size : 2 * size]
    outs = refs[2 * size :]
    place = place_ref[0]
    flag = flag_of(keep_ref, count, partner_of(place) if swapped else place, place)
    for c, heads in enumerate(chunks):
        dq_ref, dkv_ref = outs[2 * c : 2 * c + 2]

        @pl.when(flag)
        def _(c=c, heads=heads, dq_ref=dq_ref, dkv_ref=dkv_ref):
            dq, dk, dv = task(
                read_queries(x_refs[c : c + 1], heads, head_dim), read_keys(kv_refs[c], heads, head_dim), factor
            )
            dq_ref[...] = join(dq).astype(dq_ref.dtype)
            dkv_ref[...] = join(dk + dv)

        @pl.when(jnp.logical_not(flag))
        def _(dq_ref=dq_ref, dkv_ref=dkv_ref):
            dq_ref[...] = jnp.zeros_like(dq_ref)
            dkv_ref[...] = jnp.zeros_like(dkv_ref)


def far_kernel(heads, head_dim, factor, count, level, first, keep_ref, place_ref, x_ref, *refs):
    c_refs, kv_ref, refs = refs[:HOPS], refs[HOPS], refs[HOPS + 1 :]
    if first:
        earlier, (dq_ref, cdq_ref, dkv_ref, acc_ref) = None, refs
    else:
        earlier, (dq_ref, cdq_ref, dkv_ref, acc_ref) = refs[:2], refs[2:]
    place = place_ref[0]
    jump = jnp.where(lax.rem(place, 4) < 2, 2, -2)
    target = place + 2 * jump if level else place
    acc_ref[...] = jnp.zeros_like(acc_ref)
    slots = ((place + jump, (x_ref,), dq_ref), (partner_of(place) + jump, c_refs, cdq_ref))
    for i, (query, queries_ref, out_ref) in enumerate(slots):
        flag = flag_of(keep_ref, count, query, target)

        @pl.when(flag)
        def _(i=i, queries_ref=queries_ref, out_ref=out_ref):
            dq, dk, dv = task(
                read_queries(queries_ref, heads, head_dim), read_keys(kv_ref, heads, head_dim), factor
            )
            total = join(dq) if first else earlier[i][...] + join(dq)
            out_ref[...] = total.astype(out_ref.dtype)
            acc_ref[...] += join(dk + dv)

        @pl.when(jnp.logical_not(flag))
        def _(i=i, out_ref=out_ref):
            if first:
                out_ref[...] = jnp.zeros_like(out_ref)
            else:
                out_ref[...] = earlier[i][...].astype(out_ref.dtype)

    dkv_ref[...] = acc_ref[...].astype(dkv_ref.dtype)


def finish_kernel(chunks, head_dim, scale, *refs):
    ins, outs = refs[:-3], refs[-3:]
    groups = [ins[i * 7 : (i + 1) * 7] for i in range(len(chunks))]
    dq_all, dk_all, dv_all = [], [], []
    for heads, group in zip(chunks, groups):
        dq_own, dq_core, dq_far, dkv_own, dkv_core, dkv_far, zdkv = group
        rows = heads * head_dim
        dq = dq_own[...] + dq_core[...].astype(F32) + dq_far[...].astype(F32)
        total = dkv_own[...] + dkv_core[...] + dkv_far[...] + zdkv[...].astype(F32)
        dq_all.append((dq * scale).astype(BF16))
        dk_all.append((total[:rows] * scale).astype(BF16))
        dv_all.append(total[rows:].astype(BF16))
    for parts, ref in zip((dq_all, dk_all, dv_all), outs):
        ref[...] = join(parts).T


def per_device(query_rows, key_rows, value_rows, out_rows, grad_out, normalizer, keep_tasks):
    tokens, width = query_rows.shape
    head_dim = width // HEADS
    scale = head_dim ** (-0.5)
    factor = scale * LOG2E
    count = lax.axis_size("tok")
    chunks = CHUNK_HEADS
    place = jnp.reshape(lax.axis_index("tok"), (1,)).astype(jnp.int32)

    def send(value, pairs):
        return lax.ppermute(value, "tok", [(a, b % count) for a, b in pairs])

    everyone = range(count)
    across = [(i, i ^ 2) for i in everyone]
    core = [(i, i ^ 1) for i in everyone]
    level_in = [(i, i - 4 if i % 4 < 2 else i + 4) for i in everyone]
    level_out = [(i, i + 4 if i % 4 < 2 else i - 4) for i in everyone]

    def shape(rows, dtype):
        return jax.ShapeDtypeStruct((rows, tokens), dtype)

    x_rows = [2 * h * head_dim + extra_rows(h) for h in chunks]
    hbm = pl.BlockSpec(memory_space=pltpu.HBM)
    fixed = lambda *values: [pltpu.with_memory_space_constraint(v, pltpu.HBM) for v in values]
    x_own = pl.pallas_call(
        functools.partial(pack_queries, chunks, head_dim),
        out_shape=[shape(n, BF16) for n in x_rows],
        in_specs=[hbm] * 4,
        out_specs=[VMEM] * len(chunks),
        scratch_shapes=[pltpu.VMEM((tokens, width), BF16)] * 3
        + [pltpu.VMEM((HEADS, tokens), F32), pltpu.SemaphoreType.DMA((4,))],
        compiler_params=params(),
        name="pack_queries",
    )(*fixed(query_rows, grad_out, out_rows, normalizer))
    kv_own = pl.pallas_call(
        functools.partial(pack_keys, chunks, head_dim),
        out_shape=[shape(2 * h * head_dim, BF16) for h in chunks],
        in_specs=[hbm] * 2 + [pl.BlockSpec(memory_space=pl.ANY)],
        out_specs=[VMEM] * len(chunks),
        scratch_shapes=[pltpu.VMEM((tokens, width), BF16)] * 2 + [pltpu.SemaphoreType.DMA((2,))],
        compiler_params=params(),
        name="pack_keys",
    )(*fixed(key_rows, value_rows), x_own[0])
    x_far = [send(x, across) for x in x_own]
    kv_level = [send(kv, level_in) for kv in kv_own]
    x_core = [send(x, core) for x in x_own]

    def work_of(heads):
        return 10 * tokens * tokens * 256 * heads

    def near(swapped, xs, dq_type, share):
        out = []
        for heads in chunks:
            rows = heads * head_dim
            out += [shape(rows, dq_type), shape(2 * rows, F32)]
        got = pl.pallas_call(
            functools.partial(near_kernel, chunks, head_dim, factor, count, swapped),
            out_shape=out,
            in_specs=[SMEM] * 2 + [VMEM] * (2 * len(chunks)),
            out_specs=[VMEM] * len(out),
            compiler_params=params(),
            cost_estimate=cost(int(work_of(HEADS) * share), 1024),
            name="near_tasks",
        )(keep_tasks, place, *xs, *kv_own)
        return got[::2], got[1::2]

    def far(c, level, x, hop, keys, earlier):
        rows = chunks[c] * head_dim
        dq_type = BF16 if earlier else F32
        return pl.pallas_call(
            functools.partial(far_kernel, chunks[c], head_dim, factor, count, level, not earlier),
            out_shape=[shape(rows, dq_type)] * 2 + [shape(2 * rows, BF16 if level else F32)],
            in_specs=[SMEM] * 2 + [VMEM] * (2 + HOPS + len(earlier)),
            out_specs=[VMEM] * 3,
            scratch_shapes=[pltpu.VMEM((2 * rows, tokens), F32)],
            compiler_params=params(),
            cost_estimate=cost(int(work_of(chunks[c]) * FAR_COST), 1024),
            name="far_tasks",
        )(keep_tasks, place, x, *hop, keys, *earlier)

    done = x_core[0]
    far_out = []
    for c in range(len(chunks)):
        x = after(x_far[c], done)
        cuts = [2 * chunks[c] * i // HOPS * head_dim for i in range(HOPS)] + [x.shape[0]]
        cuts = [-(-cut // head_dim) * head_dim for cut in cuts]
        hop = [send(x[i:j], core) for i, j in zip(cuts, cuts[1:])]
        dq_x, dq_c, dkv_far = far(c, False, x, hop, kv_own[c], ())
        z = after(kv_level[c], dq_x)
        dq_x, dq_c, zdkv = far(c, True, x, hop, z, (dq_x, dq_c))
        done = dq_x
        dq_far = (dq_x.astype(F32) + send(dq_c, core).astype(F32)).astype(BF16)
        far_out.append((send(dq_far, across), dkv_far, send(zdkv, level_out)))
    dq_core, dkv_core = near(True, [after(value, done) for value in x_core], BF16, CORE_COST)
    done = dq_core[0]
    dq_own, dkv_own = near(False, [after(x, done, far_out[0][2]) for x in x_own], F32, SELF_COST)
    finish_args = []
    for c in range(len(chunks)):
        dq_far, dkv_far, zdkv = far_out[c]
        finish_args += [
            dq_own[c],
            send(dq_core[c], core),
            dq_far,
            dkv_own[c],
            dkv_core[c],
            dkv_far,
            zdkv,
        ]
    grad_query, grad_key, grad_value = pl.pallas_call(
        functools.partial(finish_kernel, chunks, head_dim, scale),
        out_shape=[jax.ShapeDtypeStruct((tokens, width), BF16)] * 3,
        in_specs=[VMEM] * len(finish_args),
        out_specs=[VMEM] * 3,
        compiler_params=params(),
        name="finish",
    )(*finish_args)
    return grad_query, grad_key, grad_value


def solution(mesh):
    rows = P(("groups", "tok"), None)
    return jax.shard_map(
        per_device,
        mesh=mesh,
        in_specs=(rows, rows, rows, rows, rows, P(None, ("groups", "tok")), P("groups", None)),
        out_specs=(rows, rows, rows),
        check_vma=False,
    )
```

```python
import functools
import math

import jax
import jax.numpy as jnp
from jax import lax
from jax.experimental import pallas as pl
from jax.experimental.pallas import tpu as pltpu
from jax.sharding import PartitionSpec as P

HEADS = 16
RADIUS = 2
WIN = 5
PARTS = 3
CHUNK_HEADS = (8, 8)
HOPS = 2
AHEAD = 2
CORE_COST, FAR_COST, SELF_COST = (0.01, 0.01, 0.01)
NN = (((1,), (0,)), ((), ()))
NT = (((1,), (1,)), ((), ()))
TN = (((0,), (0,)), ((), ()))
LOG2E = math.log2(math.e)
F32 = jnp.float32
BF16 = jnp.bfloat16
VMEM = pl.BlockSpec(memory_space=pltpu.VMEM)
SMEM = pl.BlockSpec(memory_space=pltpu.SMEM)


def dot(left, right, dims):
    return lax.dot_general(left, right, dims, preferred_element_type=F32)


def join(parts):
    return jnp.concatenate(parts, axis=0)


def params(mib=24):
    return pltpu.CompilerParams(vmem_limit_bytes=mib * 1024 * 1024)


def after(value, *tokens):
    return lax.optimization_barrier((value,) + tokens)[0]


def cost(flops, size):
    return pl.CostEstimate(flops=flops, bytes_accessed=size, transcendentals=0)


def split_parts(value):
    out = []
    for _ in range(PARTS):
        piece = value.astype(BF16)
        out.append(piece)
        value = value - piece.astype(F32)
    return out


def extra_rows(heads):
    return -(-2 * PARTS * heads // 16) * 16


def pack_kernel(chunks, head_dim, q_hbm, do_hbm, o_hbm, lse_hbm, k_hbm, v_hbm, *rest):
    count = len(chunks)
    x_refs, kv_refs = rest[:count], rest[count : 2 * count]
    q_ref, do_ref, o_ref, lse_ref, k_ref, v_ref, sems = rest[2 * count :]
    sources = (q_hbm, do_hbm, o_hbm, lse_hbm, k_hbm, v_hbm)
    targets = (q_ref, do_ref, o_ref, lse_ref, k_ref, v_ref)
    copies = [
        pltpu.make_async_copy(source, target, sems.at[i])
        for i, (source, target) in enumerate(zip(sources, targets))
    ]
    for copy in copies:
        copy.start()
    for copy in copies[:4]:
        copy.wait()
    lse = lse_ref[...] * LOG2E
    first = 0
    for heads, out_ref in zip(chunks, x_refs):
        rows = heads * head_dim
        span = slice(first * head_dim, first * head_dim + rows)
        do_t = do_ref[:, span].T
        out_ref[:rows] = q_ref[:, span].T
        out_ref[rows : 2 * rows] = do_t
        product = do_t.astype(F32) * o_ref[:, span].T.astype(F32)
        delta = [
            jnp.sum(product[h * head_dim : (h + 1) * head_dim], axis=0, keepdims=True)
            for h in range(heads)
        ]
        pieces = split_parts(join([lse[first : first + heads]] + delta))
        pad = extra_rows(heads) - 2 * PARTS * heads
        if pad:
            pieces.append(jnp.zeros((pad, lse.shape[1]), BF16))
        out_ref[2 * rows :] = join([piece.astype(F32) for piece in pieces]).astype(BF16)
        first += heads
    for copy in copies[4:]:
        copy.wait()
    first = 0
    for heads, out_ref in zip(chunks, kv_refs):
        rows = heads * head_dim
        span = slice(first * head_dim, first * head_dim + rows)
        out_ref[:rows] = k_ref[:, span].T
        out_ref[rows:] = v_ref[:, span].T
        first += heads


def read_queries(x_refs, heads, head_dim):
    blocks = []
    for ref in x_refs:
        blocks += [ref[i : i + head_dim] for i in range(0, 2 * heads * head_dim, head_dim) if i < ref.shape[0]]
    q, do = blocks[:heads], blocks[heads : 2 * heads]
    extra = x_refs[-1][-extra_rows(heads) :].astype(F32)
    step = 2 * heads
    total = extra[:step]
    for i in range(1, PARTS):
        total = total + extra[i * step : (i + 1) * step]
    lse = [total[h : h + 1] for h in range(heads)]
    delta = [total[heads + h : heads + h + 1] for h in range(heads)]
    return q, do, lse, delta


def read_keys(ref, heads, head_dim):
    rows = heads * head_dim
    k = [ref[h * head_dim : (h + 1) * head_dim] for h in range(heads)]
    v = [ref[rows + h * head_dim : rows + (h + 1) * head_dim] for h in range(heads)]
    return k, v


def task(queries, keys, factor):
    q, do, lse, delta = queries
    k, v = keys
    size = len(q)
    dq, dk, dv = [], [], []
    ready = []
    for i in range(size + AHEAD):
        if i < size:
            scores = dot(k[i], q[i], TN)
            prob_grad = dot(v[i], do[i], TN)
            probs = jnp.exp2(scores * factor - lse[i])
            score_grad = (probs * (prob_grad - delta[i])).astype(BF16)
            ready.append((probs.astype(BF16), score_grad))
        if i >= AHEAD:
            h = i - AHEAD
            probs, score_grad = ready[h]
            dv.append(dot(do[h], probs, NT))
            dk.append(dot(q[h], score_grad, NT))
            dq.append(dot(k[h], score_grad, NN))
    return dq, dk, dv


def flag_of(keep_ref, count, query, key):
    offset = key - query + RADIUS
    inside = (key >= 0) & (key < count) & (offset >= 0) & (offset < WIN)
    value = keep_ref[query, jnp.clip(offset, 0, WIN - 1)]
    return inside & (value > 0)


def partner_of(place):
    return place + 1 - 2 * lax.rem(place, 2)


def near_kernel(chunks, head_dim, factor, count, swapped, keep_ref, place_ref, *refs):
    size = len(chunks)
    x_refs, kv_refs = refs[:size], refs[size : 2 * size]
    outs = refs[2 * size :]
    place = place_ref[0]
    flag = flag_of(keep_ref, count, partner_of(place) if swapped else place, place)
    for c, heads in enumerate(chunks):
        dq_ref, dkv_ref = outs[2 * c : 2 * c + 2]

        @pl.when(flag)
        def _(c=c, heads=heads, dq_ref=dq_ref, dkv_ref=dkv_ref):
            dq, dk, dv = task(
                read_queries(x_refs[c : c + 1], heads, head_dim), read_keys(kv_refs[c], heads, head_dim), factor
            )
            dq_ref[...] = join(dq).astype(dq_ref.dtype)
            dkv_ref[...] = join(dk + dv)

        @pl.when(jnp.logical_not(flag))
        def _(dq_ref=dq_ref, dkv_ref=dkv_ref):
            dq_ref[...] = jnp.zeros_like(dq_ref)
            dkv_ref[...] = jnp.zeros_like(dkv_ref)


def far_kernel(heads, head_dim, factor, count, level, first, keep_ref, place_ref, x_ref, *refs):
    c_refs, kv_ref, refs = refs[:HOPS], refs[HOPS], refs[HOPS + 1 :]
    if first:
        earlier, (dq_ref, cdq_ref, dkv_ref, acc_ref) = None, refs
    else:
        earlier, (dq_ref, cdq_ref, dkv_ref, acc_ref) = refs[:2], refs[2:]
    place = place_ref[0]
    jump = jnp.where(lax.rem(place, 4) < 2, 2, -2)
    target = place + 2 * jump if level else place
    acc_ref[...] = jnp.zeros_like(acc_ref)
    slots = ((place + jump, (x_ref,), dq_ref), (partner_of(place) + jump, c_refs, cdq_ref))
    for i, (query, queries_ref, out_ref) in enumerate(slots):
        flag = flag_of(keep_ref, count, query, target)

        @pl.when(flag)
        def _(i=i, queries_ref=queries_ref, out_ref=out_ref):
            dq, dk, dv = task(
                read_queries(queries_ref, heads, head_dim), read_keys(kv_ref, heads, head_dim), factor
            )
            total = join(dq) if first else earlier[i][...] + join(dq)
            out_ref[...] = total.astype(out_ref.dtype)
            acc_ref[...] += join(dk + dv)

        @pl.when(jnp.logical_not(flag))
        def _(i=i, out_ref=out_ref):
            if first:
                out_ref[...] = jnp.zeros_like(out_ref)
            else:
                out_ref[...] = earlier[i][...].astype(out_ref.dtype)

    dkv_ref[...] = acc_ref[...].astype(dkv_ref.dtype)


def finish_kernel(chunks, head_dim, scale, *refs):
    ins, outs = refs[:-3], refs[-3:]
    groups = [ins[i * 7 : (i + 1) * 7] for i in range(len(chunks))]
    dq_all, dk_all, dv_all = [], [], []
    for heads, group in zip(chunks, groups):
        dq_own, dq_core, dq_far, dkv_own, dkv_core, dkv_far, zdkv = group
        rows = heads * head_dim
        dq = dq_own[...] + dq_core[...].astype(F32) + dq_far[...].astype(F32)
        total = dkv_own[...] + dkv_core[...] + dkv_far[...] + zdkv[...].astype(F32)
        dq_all.append((dq * scale).astype(BF16))
        dk_all.append((total[:rows] * scale).astype(BF16))
        dv_all.append(total[rows:].astype(BF16))
    for parts, ref in zip((dq_all, dk_all, dv_all), outs):
        ref[...] = join(parts).T


def per_device(query_rows, key_rows, value_rows, out_rows, grad_out, normalizer, keep_tasks):
    tokens, width = query_rows.shape
    head_dim = width // HEADS
    scale = head_dim ** (-0.5)
    factor = scale * LOG2E
    count = lax.axis_size("tok")
    chunks = CHUNK_HEADS
    place = jnp.reshape(lax.axis_index("tok"), (1,)).astype(jnp.int32)

    def send(value, pairs):
        return lax.ppermute(value, "tok", [(a, b % count) for a, b in pairs])

    everyone = range(count)
    across = [(i, i ^ 2) for i in everyone]
    core = [(i, i ^ 1) for i in everyone]
    level_in = [(i, i - 4 if i % 4 < 2 else i + 4) for i in everyone]
    level_out = [(i, i + 4 if i % 4 < 2 else i - 4) for i in everyone]

    def shape(rows, dtype):
        return jax.ShapeDtypeStruct((rows, tokens), dtype)

    x_rows = [2 * h * head_dim + extra_rows(h) for h in chunks]
    packed = pl.pallas_call(
        functools.partial(pack_kernel, chunks, head_dim),
        out_shape=[shape(n, BF16) for n in x_rows] + [shape(2 * h * head_dim, BF16) for h in chunks],
        in_specs=[pl.BlockSpec(memory_space=pltpu.HBM)] * 6,
        out_specs=[VMEM] * (2 * len(chunks)),
        scratch_shapes=[pltpu.VMEM((tokens, width), BF16)] * 3
        + [pltpu.VMEM((HEADS, tokens), F32)]
        + [pltpu.VMEM((tokens, width), BF16)] * 2
        + [pltpu.SemaphoreType.DMA((6,))],
        compiler_params=params(),
        name="pack",
    )(
        *[
            pltpu.with_memory_space_constraint(value, pltpu.HBM)
            for value in (query_rows, grad_out, out_rows, normalizer, key_rows, value_rows)
        ]
    )
    x_own, kv_own = packed[: len(chunks)], packed[len(chunks) :]
    x_far = [send(x, across) for x in x_own]
    kv_level = [send(kv, level_in) for kv in kv_own]
    x_core = [send(x, core) for x in x_own]

    def work_of(heads):
        return 10 * tokens * tokens * 256 * heads

    def near(swapped, xs, dq_type, share):
        out = []
        for heads in chunks:
            rows = heads * head_dim
            out += [shape(rows, dq_type), shape(2 * rows, F32)]
        got = pl.pallas_call(
            functools.partial(near_kernel, chunks, head_dim, factor, count, swapped),
            out_shape=out,
            in_specs=[SMEM] * 2 + [VMEM] * (2 * len(chunks)),
            out_specs=[VMEM] * len(out),
            compiler_params=params(),
            cost_estimate=cost(int(work_of(HEADS) * share), 1024),
            name="near_tasks",
        )(keep_tasks, place, *xs, *kv_own)
        return got[::2], got[1::2]

    def far(c, level, x, hop, keys, earlier):
        rows = chunks[c] * head_dim
        dq_type = BF16 if earlier else F32
        return pl.pallas_call(
            functools.partial(far_kernel, chunks[c], head_dim, factor, count, level, not earlier),
            out_shape=[shape(rows, dq_type)] * 2 + [shape(2 * rows, BF16 if level else F32)],
            in_specs=[SMEM] * 2 + [VMEM] * (2 + HOPS + len(earlier)),
            out_specs=[VMEM] * 3,
            scratch_shapes=[pltpu.VMEM((2 * rows, tokens), F32)],
            compiler_params=params(),
            cost_estimate=cost(int(work_of(chunks[c]) * FAR_COST), 1024),
            name="far_tasks",
        )(keep_tasks, place, x, *hop, keys, *earlier)

    done = x_core[0]
    far_out = []
    for c in range(len(chunks)):
        x = after(x_far[c], done)
        cuts = [2 * chunks[c] * i // HOPS * head_dim for i in range(HOPS)] + [x.shape[0]]
        cuts = [-(-cut // head_dim) * head_dim for cut in cuts]
        hop = [send(x[i:j], core) for i, j in zip(cuts, cuts[1:])]
        dq_x, dq_c, dkv_far = far(c, False, x, hop, kv_own[c], ())
        z = after(kv_level[c], dq_x)
        dq_x, dq_c, zdkv = far(c, True, x, hop, z, (dq_x, dq_c))
        done = dq_x
        dq_far = (dq_x.astype(F32) + send(dq_c, core).astype(F32)).astype(BF16)
        far_out.append((send(dq_far, across), dkv_far, send(zdkv, level_out)))
    dq_core, dkv_core = near(True, [after(value, done) for value in x_core], BF16, CORE_COST)
    done = dq_core[0]
    dq_own, dkv_own = near(False, [after(x, done, far_out[0][2]) for x in x_own], F32, SELF_COST)
    finish_args = []
    for c in range(len(chunks)):
        dq_far, dkv_far, zdkv = far_out[c]
        finish_args += [
            dq_own[c],
            send(dq_core[c], core),
            dq_far,
            dkv_own[c],
            dkv_core[c],
            dkv_far,
            zdkv,
        ]
    grad_query, grad_key, grad_value = pl.pallas_call(
        functools.partial(finish_kernel, chunks, head_dim, scale),
        out_shape=[jax.ShapeDtypeStruct((tokens, width), BF16)] * 3,
        in_specs=[VMEM] * len(finish_args),
        out_specs=[VMEM] * 3,
        compiler_params=params(),
        name="finish",
    )(*finish_args)
    return grad_query, grad_key, grad_value


def solution(mesh):
    rows = P(("groups", "tok"), None)
    return jax.shard_map(
        per_device,
        mesh=mesh,
        in_specs=(rows, rows, rows, rows, rows, P(None, ("groups", "tok")), P("groups", None)),
        out_specs=(rows, rows, rows),
        check_vma=False,
    )
```

```python
import functools
import math

import jax
import jax.numpy as jnp
from jax import lax
from jax.experimental import pallas as pl
from jax.experimental.pallas import tpu as pltpu
from jax.sharding import PartitionSpec as P

HEADS = 16
RADIUS = 2
WIN = 5
PARTS = 3
CHUNK_HEADS = (8, 8)
HOPS = 2
AHEAD = 2
CORE_COST, FAR_COST, SELF_COST = (0.01, 0.01, 0.01)
NN = (((1,), (0,)), ((), ()))
NT = (((1,), (1,)), ((), ()))
TN = (((0,), (0,)), ((), ()))
LOG2E = math.log2(math.e)
F32 = jnp.float32
BF16 = jnp.bfloat16
VMEM = pl.BlockSpec(memory_space=pltpu.VMEM)
SMEM = pl.BlockSpec(memory_space=pltpu.SMEM)


def dot(left, right, dims):
    return lax.dot_general(left, right, dims, preferred_element_type=F32)


def join(parts):
    return jnp.concatenate(parts, axis=0)


def params(mib=16):
    return pltpu.CompilerParams(vmem_limit_bytes=mib * 1024 * 1024)


def after(value, *tokens):
    return lax.optimization_barrier((value,) + tokens)[0]


def cost(flops, size):
    return pl.CostEstimate(flops=flops, bytes_accessed=size, transcendentals=0)


def split_parts(value):
    out = []
    for _ in range(PARTS):
        piece = value.astype(BF16)
        out.append(piece)
        value = value - piece.astype(F32)
    return out


def extra_rows(heads):
    return -(-2 * PARTS * heads // 16) * 16


def fetch(sources, targets, sems):
    copies = [
        pltpu.make_async_copy(source, target, sems.at[i])
        for i, (source, target) in enumerate(zip(sources, targets))
    ]
    for copy in copies:
        copy.start()
    for copy in copies:
        copy.wait()


def pack_queries(first, heads, head_dim, q_hbm, do_hbm, o_hbm, lse_hbm, *rest):
    out_ref, q_ref, do_ref, o_ref, lse_ref, sems = rest[-6:]
    rows = heads * head_dim
    span = pl.ds(first * head_dim, rows)
    sources = [ref.at[:, span] for ref in (q_hbm, do_hbm, o_hbm)] + [lse_hbm]
    fetch(sources, (q_ref, do_ref, o_ref, lse_ref), sems)
    do_t = do_ref[...].T
    out_ref[:rows] = q_ref[...].T
    out_ref[rows : 2 * rows] = do_t
    product = do_t.astype(F32) * o_ref[...].T.astype(F32)
    delta = [
        jnp.sum(product[h * head_dim : (h + 1) * head_dim], axis=0, keepdims=True)
        for h in range(heads)
    ]
    pieces = split_parts(join([lse_ref[first : first + heads] * LOG2E] + delta))
    pad = extra_rows(heads) - 2 * PARTS * heads
    if pad:
        pieces.append(jnp.zeros((pad, out_ref.shape[1]), BF16))
    out_ref[2 * rows :] = join([piece.astype(F32) for piece in pieces]).astype(BF16)


def pack_keys(chunks, head_dim, k_hbm, v_hbm, token_ref, *rest):
    kv_refs, (k_ref, v_ref, sems) = rest[: len(chunks)], rest[len(chunks) :]
    fetch((k_hbm, v_hbm), (k_ref, v_ref), sems)
    first = 0
    for heads, out_ref in zip(chunks, kv_refs):
        rows = heads * head_dim
        span = slice(first * head_dim, first * head_dim + rows)
        out_ref[:rows] = k_ref[:, span].T
        out_ref[rows:] = v_ref[:, span].T
        first += heads


def read_queries(x_refs, heads, head_dim):
    blocks = []
    for ref in x_refs:
        blocks += [ref[i : i + head_dim] for i in range(0, 2 * heads * head_dim, head_dim) if i < ref.shape[0]]
    q, do = blocks[:heads], blocks[heads : 2 * heads]
    extra = x_refs[-1][-extra_rows(heads) :].astype(F32)
    step = 2 * heads
    total = extra[:step]
    for i in range(1, PARTS):
        total = total + extra[i * step : (i + 1) * step]
    lse = [total[h : h + 1] for h in range(heads)]
    delta = [total[heads + h : heads + h + 1] for h in range(heads)]
    return q, do, lse, delta


def read_keys(ref, heads, head_dim):
    rows = heads * head_dim
    k = [ref[h * head_dim : (h + 1) * head_dim] for h in range(heads)]
    v = [ref[rows + h * head_dim : rows + (h + 1) * head_dim] for h in range(heads)]
    return k, v


def task(queries, keys, factor):
    q, do, lse, delta = queries
    k, v = keys
    size = len(q)
    dq, dk, dv = [], [], []
    ready = []
    for i in range(size + AHEAD):
        if i < size:
            scores = dot(k[i], q[i], TN)
            prob_grad = dot(v[i], do[i], TN)
            probs = jnp.exp2(scores * factor - lse[i])
            score_grad = (probs * (prob_grad - delta[i])).astype(BF16)
            ready.append((probs.astype(BF16), score_grad))
        if i >= AHEAD:
            h = i - AHEAD
            probs, score_grad = ready[h]
            dv.append(dot(do[h], probs, NT))
            dk.append(dot(q[h], score_grad, NT))
            dq.append(dot(k[h], score_grad, NN))
    return dq, dk, dv


def flag_of(keep_ref, count, query, key):
    offset = key - query + RADIUS
    inside = (key >= 0) & (key < count) & (offset >= 0) & (offset < WIN)
    value = keep_ref[query, jnp.clip(offset, 0, WIN - 1)]
    return inside & (value > 0)


def split_kernel(x_ref, *out_refs):
    first = 0
    for out_ref in out_refs:
        out_ref[...] = x_ref[first : first + out_ref.shape[0]]
        first += out_ref.shape[0]


def partner_of(place):
    return place + 1 - 2 * lax.rem(place, 2)


def near_kernel(chunks, head_dim, factor, count, swapped, keep_ref, place_ref, *refs):
    size = len(chunks)
    x_refs, kv_refs = refs[:size], refs[size : 2 * size]
    outs = refs[2 * size :]
    place = place_ref[0]
    flag = flag_of(keep_ref, count, partner_of(place) if swapped else place, place)
    for c, heads in enumerate(chunks):
        dq_ref, dkv_ref = outs[2 * c : 2 * c + 2]

        @pl.when(flag)
        def _(c=c, heads=heads, dq_ref=dq_ref, dkv_ref=dkv_ref):
            dq, dk, dv = task(
                read_queries(x_refs[c : c + 1], heads, head_dim), read_keys(kv_refs[c], heads, head_dim), factor
            )
            dq_ref[...] = join(dq).astype(dq_ref.dtype)
            dkv_ref[...] = join(dk + dv)

        @pl.when(jnp.logical_not(flag))
        def _(dq_ref=dq_ref, dkv_ref=dkv_ref):
            dq_ref[...] = jnp.zeros_like(dq_ref)
            dkv_ref[...] = jnp.zeros_like(dkv_ref)


def far_kernel(heads, head_dim, factor, count, level, first, keep_ref, place_ref, x_ref, *refs):
    c_refs, kv_ref, refs = refs[:HOPS], refs[HOPS], refs[HOPS + 1 :]
    if first:
        earlier, (dq_ref, cdq_ref, dkv_ref, acc_ref) = None, refs
    else:
        earlier, (dq_ref, cdq_ref, dkv_ref, acc_ref) = refs[:2], refs[2:]
    place = place_ref[0]
    jump = jnp.where(lax.rem(place, 4) < 2, 2, -2)
    target = place + 2 * jump if level else place
    acc_ref[...] = jnp.zeros_like(acc_ref)
    slots = ((place + jump, (x_ref,), dq_ref), (partner_of(place) + jump, c_refs, cdq_ref))
    for i, (query, queries_ref, out_ref) in enumerate(slots):
        flag = flag_of(keep_ref, count, query, target)

        @pl.when(flag)
        def _(i=i, queries_ref=queries_ref, out_ref=out_ref):
            dq, dk, dv = task(
                read_queries(queries_ref, heads, head_dim), read_keys(kv_ref, heads, head_dim), factor
            )
            total = join(dq) if first else earlier[i][...] + join(dq)
            out_ref[...] = total.astype(out_ref.dtype)
            acc_ref[...] += join(dk + dv)

        @pl.when(jnp.logical_not(flag))
        def _(i=i, out_ref=out_ref):
            if first:
                out_ref[...] = jnp.zeros_like(out_ref)
            else:
                out_ref[...] = earlier[i][...].astype(out_ref.dtype)

    dkv_ref[...] = acc_ref[...].astype(dkv_ref.dtype)


def finish_kernel(first, heads, head_dim, scale, *refs):
    dq_own, dq_core, dq_far, dkv_own, dkv_core, dkv_far, zdkv = refs[:7]
    outs, held, sems = refs[-7:-4], refs[-4:-1], refs[-1]
    rows = heads * head_dim
    dq = dq_own[...] + dq_core[...].astype(F32) + dq_far[...].astype(F32)
    total = dkv_own[...] + dkv_core[...] + dkv_far[...] + zdkv[...].astype(F32)
    values = (dq * scale, total[:rows] * scale, total[rows:])
    copies = []
    for i, (value, ref, out) in enumerate(zip(values, held, outs)):
        ref[...] = value.astype(BF16).T
        span = pl.ds(first * head_dim, rows)
        copies.append(pltpu.make_async_copy(ref, out.at[:, span], sems.at[i]))
        copies[-1].start()
    for copy in copies:
        copy.wait()


def per_device(query_rows, key_rows, value_rows, out_rows, grad_out, normalizer, keep_tasks):
    tokens, width = query_rows.shape
    head_dim = width // HEADS
    scale = head_dim ** (-0.5)
    factor = scale * LOG2E
    count = lax.axis_size("tok")
    chunks = CHUNK_HEADS
    place = jnp.reshape(lax.axis_index("tok"), (1,)).astype(jnp.int32)

    def send(value, pairs):
        return lax.ppermute(value, "tok", [(a, b % count) for a, b in pairs])

    everyone = range(count)
    across = [(i, i ^ 2) for i in everyone]
    core = [(i, i ^ 1) for i in everyone]
    level_in = [(i, i - 4 if i % 4 < 2 else i + 4) for i in everyone]
    level_out = [(i, i + 4 if i % 4 < 2 else i - 4) for i in everyone]

    def shape(rows, dtype):
        return jax.ShapeDtypeStruct((rows, tokens), dtype)

    x_rows = [2 * h * head_dim + extra_rows(h) for h in chunks]
    hbm = pl.BlockSpec(memory_space=pltpu.HBM)
    fixed = lambda *values: [pltpu.with_memory_space_constraint(v, pltpu.HBM) for v in values]
    x_own = []
    for c, heads in enumerate(chunks):
        rows = heads * head_dim
        x_own.append(
            pl.pallas_call(
                functools.partial(pack_queries, sum(chunks[:c]), heads, head_dim),
                out_shape=shape(x_rows[c], BF16),
                in_specs=[hbm] * 4 + [pl.BlockSpec(memory_space=pl.ANY)] * c,
                out_specs=VMEM,
                scratch_shapes=[pltpu.VMEM((tokens, rows), BF16)] * 3
                + [pltpu.VMEM((HEADS, tokens), F32), pltpu.SemaphoreType.DMA((4,))],
                compiler_params=params(),
                name="pack_queries",
            )(*fixed(query_rows, grad_out, out_rows, normalizer), *x_own)
        )
    kv_own = pl.pallas_call(
        functools.partial(pack_keys, chunks, head_dim),
        out_shape=[shape(2 * h * head_dim, BF16) for h in chunks],
        in_specs=[hbm] * 2 + [pl.BlockSpec(memory_space=pl.ANY)],
        out_specs=[VMEM] * len(chunks),
        scratch_shapes=[pltpu.VMEM((tokens, width), BF16)] * 2 + [pltpu.SemaphoreType.DMA((2,))],
        compiler_params=params(),
        name="pack_keys",
    )(*fixed(key_rows, value_rows), x_own[-1])
    x_far = [send(x, across) for x in x_own]
    kv_level = [send(kv, level_in) for kv in kv_own]
    x_core = [send(x, core) for x in x_own]

    def work_of(heads):
        return 10 * tokens * tokens * 256 * heads

    def near(swapped, xs, dq_type, share):
        out = []
        for heads in chunks:
            rows = heads * head_dim
            out += [shape(rows, dq_type), shape(2 * rows, F32)]
        got = pl.pallas_call(
            functools.partial(near_kernel, chunks, head_dim, factor, count, swapped),
            out_shape=out,
            in_specs=[SMEM] * 2 + [VMEM] * (2 * len(chunks)),
            out_specs=[VMEM] * len(out),
            compiler_params=params(),
            cost_estimate=cost(int(work_of(HEADS) * share), 1024),
            name="near_tasks",
        )(keep_tasks, place, *xs, *kv_own)
        return got[::2], got[1::2]

    def far(c, level, x, hop, keys, earlier):
        rows = chunks[c] * head_dim
        dq_type = BF16 if earlier else F32
        return pl.pallas_call(
            functools.partial(far_kernel, chunks[c], head_dim, factor, count, level, not earlier),
            out_shape=[shape(rows, dq_type)] * 2 + [shape(2 * rows, BF16 if level else F32)],
            in_specs=[SMEM] * 2 + [VMEM] * (2 + HOPS + len(earlier)),
            out_specs=[VMEM] * 3,
            scratch_shapes=[pltpu.VMEM((2 * rows, tokens), F32)],
            compiler_params=params(),
            cost_estimate=cost(int(work_of(chunks[c]) * FAR_COST), 1024),
            name="far_tasks",
        )(keep_tasks, place, x, *hop, keys, *earlier)

    done = x_core[0]
    far_out = []
    for c in range(len(chunks)):
        x = after(x_far[c], done)
        hop = [send(piece, core) for piece in pl.pallas_call(
            split_kernel,
            out_shape=[
                pltpu.VMEM((chunks[c] * head_dim, tokens), BF16),
                pltpu.VMEM((x.shape[0] - chunks[c] * head_dim, tokens), BF16),
            ],
            in_specs=[VMEM],
            out_specs=[VMEM] * HOPS,
            compiler_params=params(),
            cost_estimate=cost(1024, 1024),
            name="split",
        )(x)]
        dq_x, dq_c, dkv_far = far(c, False, x, hop, kv_own[c], ())
        z = after(kv_level[c], dq_x)
        dq_x, dq_c, zdkv = far(c, True, x, hop, z, (dq_x, dq_c))
        done = dq_x
        dq_far = (dq_x.astype(F32) + send(dq_c, core).astype(F32)).astype(BF16)
        far_out.append((send(dq_far, across), dkv_far, send(zdkv, level_out)))
    dq_core, dkv_core = near(True, [after(value, done) for value in x_core], BF16, CORE_COST)
    done = dq_core[0]
    dq_own, dkv_own = near(False, [after(x, done, far_out[0][2]) for x in x_own], F32, SELF_COST)
    out = ()
    any_space = pl.BlockSpec(memory_space=pl.ANY)
    for c, heads in enumerate(chunks):
        rows = heads * head_dim
        dq_far, dkv_far, zdkv = far_out[c]
        args = (dq_own[c], send(dq_core[c], core), dq_far, dkv_own[c], dkv_core[c], dkv_far, zdkv)
        out = pl.pallas_call(
            functools.partial(finish_kernel, sum(chunks[:c]), heads, head_dim, scale),
            out_shape=[jax.ShapeDtypeStruct((tokens, width), BF16)] * 3,
            in_specs=[VMEM] * 7 + [any_space] * len(out),
            out_specs=[any_space] * 3,
            scratch_shapes=[pltpu.VMEM((tokens, rows), BF16)] * 3 + [pltpu.SemaphoreType.DMA((3,))],
            input_output_aliases={7 + i: i for i in range(len(out))},
            compiler_params=params(),
            cost_estimate=cost(1024, 1024),
            name="finish",
        )(*args, *out)
    return tuple(out)


def solution(mesh):
    rows = P(("groups", "tok"), None)
    return jax.shard_map(
        per_device,
        mesh=mesh,
        in_specs=(rows, rows, rows, rows, rows, P(None, ("groups", "tok")), P("groups", None)),
        out_specs=(rows, rows, rows),
        check_vma=False,
    )
```

```python
import functools
import math

import jax
import jax.numpy as jnp
from jax import lax
from jax.experimental import pallas as pl
from jax.experimental.pallas import tpu as pltpu
from jax.sharding import PartitionSpec as P

HEADS = 16
RADIUS = 2
WIN = 5
PARTS = 3
CHUNK_HEADS = (8, 8)
HOPS = 2
AHEAD = 2
CORE_COST, FAR_COST, SELF_COST = (0.01, 0.01, 0.01)
NN = (((1,), (0,)), ((), ()))
NT = (((1,), (1,)), ((), ()))
TN = (((0,), (0,)), ((), ()))
LOG2E = math.log2(math.e)
F32 = jnp.float32
BF16 = jnp.bfloat16
VMEM = pl.BlockSpec(memory_space=pltpu.VMEM)
SMEM = pl.BlockSpec(memory_space=pltpu.SMEM)


def dot(left, right, dims):
    return lax.dot_general(left, right, dims, preferred_element_type=F32)


def join(parts):
    return jnp.concatenate(parts, axis=0)


def params(mib=16):
    return pltpu.CompilerParams(vmem_limit_bytes=mib * 1024 * 1024)


def after(value, *tokens):
    return lax.optimization_barrier((value,) + tokens)[0]


def cost(flops, size):
    return pl.CostEstimate(flops=flops, bytes_accessed=size, transcendentals=0)


def split_parts(value):
    out = []
    for _ in range(PARTS):
        piece = value.astype(BF16)
        out.append(piece)
        value = value - piece.astype(F32)
    return out


def extra_rows(heads):
    return -(-2 * PARTS * heads // 16) * 16


def fetch(sources, targets, sems):
    copies = [
        pltpu.make_async_copy(source, target, sems.at[i])
        for i, (source, target) in enumerate(zip(sources, targets))
    ]
    for copy in copies:
        copy.start()
    for copy in copies:
        copy.wait()


def pack_queries(first, heads, head_dim, q_hbm, do_hbm, o_hbm, lse_hbm, *rest):
    out_ref, q_ref, do_ref, o_ref, lse_ref, sems = rest[-6:]
    rows = heads * head_dim
    span = pl.ds(first * head_dim, rows)
    sources = [ref.at[:, span] for ref in (q_hbm, do_hbm, o_hbm)] + [lse_hbm]
    fetch(sources, (q_ref, do_ref, o_ref, lse_ref), sems)
    do_t = do_ref[...].T
    out_ref[:rows] = q_ref[...].T
    out_ref[rows : 2 * rows] = do_t
    product = do_t.astype(F32) * o_ref[...].T.astype(F32)
    delta = [
        jnp.sum(product[h * head_dim : (h + 1) * head_dim], axis=0, keepdims=True)
        for h in range(heads)
    ]
    pieces = split_parts(join([lse_ref[first : first + heads] * LOG2E] + delta))
    pad = extra_rows(heads) - 2 * PARTS * heads
    if pad:
        pieces.append(jnp.zeros((pad, out_ref.shape[1]), BF16))
    out_ref[2 * rows :] = join([piece.astype(F32) for piece in pieces]).astype(BF16)


def pack_keys(chunks, head_dim, k_hbm, v_hbm, token_ref, *rest):
    kv_refs, (k_ref, v_ref, sems) = rest[: len(chunks)], rest[len(chunks) :]
    fetch((k_hbm, v_hbm), (k_ref, v_ref), sems)
    first = 0
    for heads, out_ref in zip(chunks, kv_refs):
        rows = heads * head_dim
        span = slice(first * head_dim, first * head_dim + rows)
        out_ref[:rows] = k_ref[:, span].T
        out_ref[rows:] = v_ref[:, span].T
        first += heads


def read_queries(x_refs, heads, head_dim):
    blocks = []
    for ref in x_refs:
        blocks += [ref[i : i + head_dim] for i in range(0, 2 * heads * head_dim, head_dim) if i < ref.shape[0]]
    q, do = blocks[:heads], blocks[heads : 2 * heads]
    extra = x_refs[-1][-extra_rows(heads) :].astype(F32)
    step = 2 * heads
    total = extra[:step]
    for i in range(1, PARTS):
        total = total + extra[i * step : (i + 1) * step]
    lse = [total[h : h + 1] for h in range(heads)]
    delta = [total[heads + h : heads + h + 1] for h in range(heads)]
    return q, do, lse, delta


def read_keys(ref, heads, head_dim):
    rows = heads * head_dim
    k = [ref[h * head_dim : (h + 1) * head_dim] for h in range(heads)]
    v = [ref[rows + h * head_dim : rows + (h + 1) * head_dim] for h in range(heads)]
    return k, v


def task(queries, keys, factor):
    q, do, lse, delta = queries
    k, v = keys
    size = len(q)
    dq, dk, dv = [], [], []
    ready = []
    for i in range(size + AHEAD):
        if i < size:
            scores = dot(k[i], q[i], TN)
            prob_grad = dot(v[i], do[i], TN)
            probs = jnp.exp2(scores * factor - lse[i])
            score_grad = (probs * (prob_grad - delta[i])).astype(BF16)
            ready.append((probs.astype(BF16), score_grad))
        if i >= AHEAD:
            h = i - AHEAD
            probs, score_grad = ready[h]
            dv.append(dot(do[h], probs, NT))
            dk.append(dot(q[h], score_grad, NT))
            dq.append(dot(k[h], score_grad, NN))
    return dq, dk, dv


def flag_of(keep_ref, count, query, key):
    offset = key - query + RADIUS
    inside = (key >= 0) & (key < count) & (offset >= 0) & (offset < WIN)
    value = keep_ref[query, jnp.clip(offset, 0, WIN - 1)]
    return inside & (value > 0)


def split_kernel(x_ref, *out_refs):
    first = 0
    for out_ref in out_refs:
        out_ref[...] = x_ref[first : first + out_ref.shape[0]]
        first += out_ref.shape[0]


def partner_of(place):
    return place + 1 - 2 * lax.rem(place, 2)


def near_kernel(chunks, head_dim, factor, count, swapped, keep_ref, place_ref, *refs):
    size = len(chunks)
    x_refs, kv_refs = refs[:size], refs[size : 2 * size]
    outs = refs[2 * size :]
    place = place_ref[0]
    flag = flag_of(keep_ref, count, partner_of(place) if swapped else place, place)
    for c, heads in enumerate(chunks):
        dq_ref, dkv_ref = outs[2 * c : 2 * c + 2]

        @pl.when(flag)
        def _(c=c, heads=heads, dq_ref=dq_ref, dkv_ref=dkv_ref):
            dq, dk, dv = task(
                read_queries(x_refs[c : c + 1], heads, head_dim), read_keys(kv_refs[c], heads, head_dim), factor
            )
            dq_ref[...] = join(dq).astype(dq_ref.dtype)
            dkv_ref[...] = join(dk + dv)

        @pl.when(jnp.logical_not(flag))
        def _(dq_ref=dq_ref, dkv_ref=dkv_ref):
            dq_ref[...] = jnp.zeros_like(dq_ref)
            dkv_ref[...] = jnp.zeros_like(dkv_ref)


def far_kernel(heads, head_dim, factor, count, level, first, keep_ref, place_ref, x_ref, *refs):
    c_refs, kv_ref, refs = refs[:HOPS], refs[HOPS], refs[HOPS + 1 :]
    if first:
        earlier, (dq_ref, cdq_ref, dkv_ref, acc_ref) = None, refs
    else:
        earlier, (dq_ref, cdq_ref, dkv_ref, acc_ref) = refs[:2], refs[2:]
    place = place_ref[0]
    jump = jnp.where(lax.rem(place, 4) < 2, 2, -2)
    target = place + 2 * jump if level else place
    sum_ref = acc_ref if level else dkv_ref
    slots = ((place + jump, (x_ref,), dq_ref), (partner_of(place) + jump, c_refs, cdq_ref))
    for i, (query, queries_ref, out_ref) in enumerate(slots):
        flag = flag_of(keep_ref, count, query, target)

        @pl.when(flag)
        def _(i=i, queries_ref=queries_ref, out_ref=out_ref):
            dq, dk, dv = task(
                read_queries(queries_ref, heads, head_dim), read_keys(kv_ref, heads, head_dim), factor
            )
            total = join(dq) if first else earlier[i][...] + join(dq)
            out_ref[...] = total.astype(out_ref.dtype)
            if i:
                sum_ref[...] += join(dk + dv)
            else:
                sum_ref[...] = join(dk + dv)

        @pl.when(jnp.logical_not(flag))
        def _(i=i, out_ref=out_ref):
            if not i:
                sum_ref[...] = jnp.zeros_like(sum_ref)
            if first:
                out_ref[...] = jnp.zeros_like(out_ref)
            else:
                out_ref[...] = earlier[i][...].astype(out_ref.dtype)

    if level:
        dkv_ref[...] = acc_ref[...].astype(dkv_ref.dtype)


def finish_kernel(first, heads, head_dim, scale, *refs):
    dq_own, dq_core, dq_far, dkv_own, dkv_core, dkv_far, zdkv = refs[:7]
    outs, held, sems = refs[-7:-4], refs[-4:-1], refs[-1]
    rows = heads * head_dim
    dq = dq_own[...] + dq_core[...].astype(F32) + dq_far[...].astype(F32)
    total = dkv_own[...] + dkv_core[...] + dkv_far[...] + zdkv[...].astype(F32)
    values = (dq * scale, total[:rows] * scale, total[rows:])
    copies = []
    for i, (value, ref, out) in enumerate(zip(values, held, outs)):
        ref[...] = value.astype(BF16).T
        span = pl.ds(first * head_dim, rows)
        copies.append(pltpu.make_async_copy(ref, out.at[:, span], sems.at[i]))
        copies[-1].start()
    for copy in copies:
        copy.wait()


def per_device(query_rows, key_rows, value_rows, out_rows, grad_out, normalizer, keep_tasks):
    tokens, width = query_rows.shape
    head_dim = width // HEADS
    scale = head_dim ** (-0.5)
    factor = scale * LOG2E
    count = lax.axis_size("tok")
    chunks = CHUNK_HEADS
    place = jnp.reshape(lax.axis_index("tok"), (1,)).astype(jnp.int32)

    def send(value, pairs):
        return lax.ppermute(value, "tok", [(a, b % count) for a, b in pairs])

    everyone = range(count)
    across = [(i, i ^ 2) for i in everyone]
    core = [(i, i ^ 1) for i in everyone]
    level_in = [(i, i - 4 if i % 4 < 2 else i + 4) for i in everyone]
    level_out = [(i, i + 4 if i % 4 < 2 else i - 4) for i in everyone]

    def shape(rows, dtype):
        return jax.ShapeDtypeStruct((rows, tokens), dtype)

    x_rows = [2 * h * head_dim + extra_rows(h) for h in chunks]
    hbm = pl.BlockSpec(memory_space=pltpu.HBM)
    fixed = lambda *values: [pltpu.with_memory_space_constraint(v, pltpu.HBM) for v in values]
    x_own = []
    for c, heads in enumerate(chunks):
        rows = heads * head_dim
        x_own.append(
            pl.pallas_call(
                functools.partial(pack_queries, sum(chunks[:c]), heads, head_dim),
                out_shape=shape(x_rows[c], BF16),
                in_specs=[hbm] * 4 + [pl.BlockSpec(memory_space=pl.ANY)] * c,
                out_specs=VMEM,
                scratch_shapes=[pltpu.VMEM((tokens, rows), BF16)] * 3
                + [pltpu.VMEM((HEADS, tokens), F32), pltpu.SemaphoreType.DMA((4,))],
                compiler_params=params(),
                name="pack_queries",
            )(*fixed(query_rows, grad_out, out_rows, normalizer), *x_own)
        )
    kv_own = pl.pallas_call(
        functools.partial(pack_keys, chunks, head_dim),
        out_shape=[shape(2 * h * head_dim, BF16) for h in chunks],
        in_specs=[hbm] * 2 + [pl.BlockSpec(memory_space=pl.ANY)],
        out_specs=[VMEM] * len(chunks),
        scratch_shapes=[pltpu.VMEM((tokens, width), BF16)] * 2 + [pltpu.SemaphoreType.DMA((2,))],
        compiler_params=params(),
        name="pack_keys",
    )(*fixed(key_rows, value_rows), x_own[-1])
    x_far = [send(x, across) for x in x_own]
    kv_level = [send(kv, level_in) for kv in kv_own]
    x_core = [send(x, core) for x in x_own]

    def work_of(heads):
        return 10 * tokens * tokens * 256 * heads

    def near(swapped, xs, dq_type, share):
        out = []
        for heads in chunks:
            rows = heads * head_dim
            out += [shape(rows, dq_type), shape(2 * rows, F32)]
        got = pl.pallas_call(
            functools.partial(near_kernel, chunks, head_dim, factor, count, swapped),
            out_shape=out,
            in_specs=[SMEM] * 2 + [VMEM] * (2 * len(chunks)),
            out_specs=[VMEM] * len(out),
            compiler_params=params(),
            cost_estimate=cost(int(work_of(HEADS) * share), 1024),
            name="near_tasks",
        )(keep_tasks, place, *xs, *kv_own)
        return got[::2], got[1::2]

    def far(c, level, x, hop, keys, earlier):
        rows = chunks[c] * head_dim
        dq_type = BF16 if earlier else F32
        return pl.pallas_call(
            functools.partial(far_kernel, chunks[c], head_dim, factor, count, level, not earlier),
            out_shape=[shape(rows, dq_type)] * 2 + [shape(2 * rows, BF16 if level else F32)],
            in_specs=[SMEM] * 2 + [VMEM] * (2 + HOPS + len(earlier)),
            out_specs=[VMEM] * 3,
            scratch_shapes=[pltpu.VMEM((2 * rows, tokens), F32)],
            compiler_params=params(),
            cost_estimate=cost(int(work_of(chunks[c]) * FAR_COST), 1024),
            name="far_tasks",
        )(keep_tasks, place, x, *hop, keys, *earlier)

    done = x_core[0]
    far_out = []
    for c in range(len(chunks)):
        x = after(x_far[c], done)
        hop = [send(piece, core) for piece in pl.pallas_call(
            split_kernel,
            out_shape=[
                pltpu.VMEM((chunks[c] * head_dim, tokens), BF16),
                pltpu.VMEM((x.shape[0] - chunks[c] * head_dim, tokens), BF16),
            ],
            in_specs=[VMEM],
            out_specs=[VMEM] * HOPS,
            compiler_params=params(),
            cost_estimate=cost(1024, 1024),
            name="split",
        )(x)]
        dq_x, dq_c, dkv_far = far(c, False, x, hop, kv_own[c], ())
        z = after(kv_level[c], dq_x)
        dq_x, dq_c, zdkv = far(c, True, x, hop, z, (dq_x, dq_c))
        done = dq_x
        dq_far = (dq_x.astype(F32) + send(dq_c, core).astype(F32)).astype(BF16)
        far_out.append((send(dq_far, across), dkv_far, send(zdkv, level_out)))
    dq_core, dkv_core = near(True, [after(value, done) for value in x_core], BF16, CORE_COST)
    done = dq_core[0]
    dq_own, dkv_own = near(False, [after(x, done, far_out[0][2]) for x in x_own], F32, SELF_COST)
    out = ()
    any_space = pl.BlockSpec(memory_space=pl.ANY)
    for c, heads in enumerate(chunks):
        rows = heads * head_dim
        dq_far, dkv_far, zdkv = far_out[c]
        args = (dq_own[c], send(dq_core[c], core), dq_far, dkv_own[c], dkv_core[c], dkv_far, zdkv)
        out = pl.pallas_call(
            functools.partial(finish_kernel, sum(chunks[:c]), heads, head_dim, scale),
            out_shape=[jax.ShapeDtypeStruct((tokens, width), BF16)] * 3,
            in_specs=[VMEM] * 7 + [any_space] * len(out),
            out_specs=[any_space] * 3,
            scratch_shapes=[pltpu.VMEM((tokens, rows), BF16)] * 3 + [pltpu.SemaphoreType.DMA((3,))],
            input_output_aliases={7 + i: i for i in range(len(out))},
            compiler_params=params(),
            cost_estimate=cost(1024, 1024),
            name="finish",
        )(*args, *out)
    return tuple(out)


def solution(mesh):
    rows = P(("groups", "tok"), None)
    return jax.shard_map(
        per_device,
        mesh=mesh,
        in_specs=(rows, rows, rows, rows, rows, P(None, ("groups", "tok")), P("groups", None)),
        out_specs=(rows, rows, rows),
        check_vma=False,
    )
```

```python
import functools
import math

import jax
import jax.numpy as jnp
from jax import lax
from jax.experimental import pallas as pl
from jax.experimental.pallas import tpu as pltpu
from jax.sharding import PartitionSpec as P

HEADS = 16
RADIUS = 2
WIN = 5
PARTS = 3
CHUNK_HEADS = (8, 8)
HOPS = 2
AHEAD = 2
CORE_COST, FAR_COST, SELF_COST = (0.01, 0.01, 0.01)
NN = (((1,), (0,)), ((), ()))
NT = (((1,), (1,)), ((), ()))
TN = (((0,), (0,)), ((), ()))
LOG2E = math.log2(math.e)
F32 = jnp.float32
BF16 = jnp.bfloat16
VMEM = pl.BlockSpec(memory_space=pltpu.VMEM)
SMEM = pl.BlockSpec(memory_space=pltpu.SMEM)


def dot(left, right, dims):
    return lax.dot_general(left, right, dims, preferred_element_type=F32)


def join(parts):
    return jnp.concatenate(parts, axis=0)


def params(mib=16):
    return pltpu.CompilerParams(vmem_limit_bytes=mib * 1024 * 1024)


def after(value, *tokens):
    return lax.optimization_barrier((value,) + tokens)[0]


def cost(flops, size):
    return pl.CostEstimate(flops=flops, bytes_accessed=size, transcendentals=0)


def split_parts(value):
    out = []
    for _ in range(PARTS):
        piece = value.astype(BF16)
        out.append(piece)
        value = value - piece.astype(F32)
    return out


def extra_rows(heads):
    return -(-2 * PARTS * heads // 16) * 16


def fetch(sources, targets, sems):
    copies = [
        pltpu.make_async_copy(source, target, sems.at[i])
        for i, (source, target) in enumerate(zip(sources, targets))
    ]
    for copy in copies:
        copy.start()
    for copy in copies:
        copy.wait()


def pack_queries(first, heads, head_dim, q_hbm, do_hbm, o_hbm, lse_hbm, *rest):
    out_ref, q_ref, do_ref, o_ref, lse_ref, sems = rest[-6:]
    rows = heads * head_dim
    span = pl.ds(first * head_dim, rows)
    sources = [ref.at[:, span] for ref in (q_hbm, do_hbm, o_hbm)] + [lse_hbm]
    fetch(sources, (q_ref, do_ref, o_ref, lse_ref), sems)
    do_t = do_ref[...].T
    out_ref[:rows] = q_ref[...].T
    out_ref[rows : 2 * rows] = do_t
    product = do_t.astype(F32) * o_ref[...].T.astype(F32)
    delta = [
        jnp.sum(product[h * head_dim : (h + 1) * head_dim], axis=0, keepdims=True)
        for h in range(heads)
    ]
    pieces = split_parts(join([lse_ref[first : first + heads] * LOG2E] + delta))
    pad = extra_rows(heads) - 2 * PARTS * heads
    if pad:
        pieces.append(jnp.zeros((pad, out_ref.shape[1]), BF16))
    out_ref[2 * rows :] = join([piece.astype(F32) for piece in pieces]).astype(BF16)


def pack_keys(chunks, head_dim, k_hbm, v_hbm, token_ref, *rest):
    kv_refs, (k_ref, v_ref, sems) = rest[: len(chunks)], rest[len(chunks) :]
    fetch((k_hbm, v_hbm), (k_ref, v_ref), sems)
    first = 0
    for heads, out_ref in zip(chunks, kv_refs):
        rows = heads * head_dim
        span = slice(first * head_dim, first * head_dim + rows)
        out_ref[:rows] = k_ref[:, span].T
        out_ref[rows:] = v_ref[:, span].T
        first += heads


def read_queries(x_refs, heads, head_dim):
    blocks = []
    for ref in x_refs:
        blocks += [ref[i : i + head_dim] for i in range(0, 2 * heads * head_dim, head_dim) if i < ref.shape[0]]
    q, do = blocks[:heads], blocks[heads : 2 * heads]
    extra = x_refs[-1][-extra_rows(heads) :].astype(F32)
    step = 2 * heads
    total = extra[:step]
    for i in range(1, PARTS):
        total = total + extra[i * step : (i + 1) * step]
    lse = [total[h : h + 1] for h in range(heads)]
    delta = [total[heads + h : heads + h + 1] for h in range(heads)]
    return q, do, lse, delta


def read_keys(ref, heads, head_dim):
    rows = heads * head_dim
    k = [ref[h * head_dim : (h + 1) * head_dim] for h in range(heads)]
    v = [ref[rows + h * head_dim : rows + (h + 1) * head_dim] for h in range(heads)]
    return k, v


def task(queries, keys, factor):
    q, do, lse, delta = queries
    k, v = keys
    size = len(q)
    dq, dk, dv = [], [], []
    ready = []
    for i in range(size + AHEAD):
        if i < size:
            scores = dot(k[i], q[i], TN)
            prob_grad = dot(v[i], do[i], TN)
            probs = jnp.exp2(scores * factor - lse[i])
            score_grad = (probs * (prob_grad - delta[i])).astype(BF16)
            ready.append((probs.astype(BF16), score_grad))
        if i >= AHEAD:
            h = i - AHEAD
            probs, score_grad = ready[h]
            dv.append(dot(do[h], probs, NT))
            dk.append(dot(q[h], score_grad, NT))
            dq.append(dot(k[h], score_grad, NN))
    return dq, dk, dv


def flag_of(keep_ref, count, query, key):
    offset = key - query + RADIUS
    inside = (key >= 0) & (key < count) & (offset >= 0) & (offset < WIN)
    value = keep_ref[query, jnp.clip(offset, 0, WIN - 1)]
    return inside & (value > 0)


def split_kernel(x_ref, *out_refs):
    first = 0
    for out_ref in out_refs:
        out_ref[...] = x_ref[first : first + out_ref.shape[0]]
        first += out_ref.shape[0]


def partner_of(place):
    return place + 1 - 2 * lax.rem(place, 2)


def near_kernel(chunks, head_dim, factor, count, swapped, keep_ref, place_ref, *refs):
    size = len(chunks)
    x_refs, kv_refs = refs[:size], refs[size : 2 * size]
    outs = refs[2 * size :]
    place = place_ref[0]
    flag = flag_of(keep_ref, count, partner_of(place) if swapped else place, place)
    for c, heads in enumerate(chunks):
        dq_ref, dkv_ref = outs[2 * c : 2 * c + 2]

        @pl.when(flag)
        def _(c=c, heads=heads, dq_ref=dq_ref, dkv_ref=dkv_ref):
            dq, dk, dv = task(
                read_queries(x_refs[c : c + 1], heads, head_dim), read_keys(kv_refs[c], heads, head_dim), factor
            )
            dq_ref[...] = join(dq).astype(dq_ref.dtype)
            dkv_ref[...] = join(dk + dv)

        @pl.when(jnp.logical_not(flag))
        def _(dq_ref=dq_ref, dkv_ref=dkv_ref):
            dq_ref[...] = jnp.zeros_like(dq_ref)
            dkv_ref[...] = jnp.zeros_like(dkv_ref)


def far_kernel(heads, head_dim, factor, count, level, first, keep_ref, place_ref, x_ref, *refs):
    c_refs, kv_ref, refs = refs[:HOPS], refs[HOPS], refs[HOPS + 1 :]
    if first:
        earlier, (dq_ref, cdq_ref, dkv_ref, acc_ref) = None, refs
    else:
        earlier, (dq_ref, cdq_ref, dkv_ref, acc_ref) = refs[:2], refs[2:]
    place = place_ref[0]
    jump = jnp.where(lax.rem(place, 4) < 2, 2, -2)
    target = place + 2 * jump if level else place
    sum_ref = acc_ref if level else dkv_ref
    slots = ((place + jump, (x_ref,), dq_ref), (partner_of(place) + jump, c_refs, cdq_ref))
    for i, (query, queries_ref, out_ref) in enumerate(slots):
        flag = flag_of(keep_ref, count, query, target)

        @pl.when(flag)
        def _(i=i, queries_ref=queries_ref, out_ref=out_ref):
            dq, dk, dv = task(
                read_queries(queries_ref, heads, head_dim), read_keys(kv_ref, heads, head_dim), factor
            )
            total = join(dq) if first else earlier[i][...] + join(dq)
            out_ref[...] = total.astype(out_ref.dtype)
            if i:
                sum_ref[...] += join(dk + dv)
            else:
                sum_ref[...] = join(dk + dv)

        @pl.when(jnp.logical_not(flag))
        def _(i=i, out_ref=out_ref):
            if not i:
                sum_ref[...] = jnp.zeros_like(sum_ref)
            if first:
                out_ref[...] = jnp.zeros_like(out_ref)
            else:
                out_ref[...] = earlier[i][...].astype(out_ref.dtype)

    if level:
        dkv_ref[...] = acc_ref[...].astype(dkv_ref.dtype)


def finish_kernel(first, heads, head_dim, scale, *refs):
    dq_own, dq_core, dq_far, dkv_own, dkv_core, dkv_far, zdkv = refs[:7]
    outs, held, sems = refs[-7:-4], refs[-4:-1], refs[-1]
    rows = heads * head_dim
    dq = dq_own[...] + dq_core[...].astype(F32) + dq_far[...].astype(F32)
    total = dkv_own[...] + dkv_core[...] + dkv_far[...] + zdkv[...].astype(F32)
    values = (dq * scale, total[:rows] * scale, total[rows:])
    copies = []
    for i, (value, ref, out) in enumerate(zip(values, held, outs)):
        ref[...] = value.astype(BF16).T
        span = pl.ds(first * head_dim, rows)
        copies.append(pltpu.make_async_copy(ref, out.at[:, span], sems.at[i]))
        copies[-1].start()
    for copy in copies:
        copy.wait()


def per_device(query_rows, key_rows, value_rows, out_rows, grad_out, normalizer, keep_tasks):
    tokens, width = query_rows.shape
    head_dim = width // HEADS
    scale = head_dim ** (-0.5)
    factor = scale * LOG2E
    count = lax.axis_size("tok")
    chunks = CHUNK_HEADS
    place = jnp.reshape(lax.axis_index("tok"), (1,)).astype(jnp.int32)

    def send(value, pairs):
        return lax.ppermute(value, "tok", [(a, b % count) for a, b in pairs])

    everyone = range(count)
    across = [(i, i ^ 2) for i in everyone]
    core = [(i, i ^ 1) for i in everyone]
    level_in = [(i, i - 4 if i % 4 < 2 else i + 4) for i in everyone]
    level_out = [(i, i + 4 if i % 4 < 2 else i - 4) for i in everyone]

    def shape(rows, dtype):
        return jax.ShapeDtypeStruct((rows, tokens), dtype)

    x_rows = [2 * h * head_dim + extra_rows(h) for h in chunks]
    hbm = pl.BlockSpec(memory_space=pltpu.HBM)
    fixed = lambda *values: [pltpu.with_memory_space_constraint(v, pltpu.HBM) for v in values]
    def queries_of(c, heads, *token):
        rows = heads * head_dim
        return pl.pallas_call(
            functools.partial(pack_queries, sum(chunks[:c]), heads, head_dim),
                out_shape=shape(x_rows[c], BF16),
                in_specs=[hbm] * 4 + [pl.BlockSpec(memory_space=pl.ANY)] * len(token),
                out_specs=VMEM,
                scratch_shapes=[pltpu.VMEM((tokens, rows), BF16)] * 3
                + [pltpu.VMEM((HEADS, tokens), F32), pltpu.SemaphoreType.DMA((4,))],
                compiler_params=params(),
                name="pack_queries",
            )(*fixed(query_rows, grad_out, out_rows, normalizer), *token)

    x_own = [queries_of(0, chunks[0])]
    kv_own = pl.pallas_call(
        functools.partial(pack_keys, chunks, head_dim),
        out_shape=[shape(2 * h * head_dim, BF16) for h in chunks],
        in_specs=[hbm] * 2 + [pl.BlockSpec(memory_space=pl.ANY)],
        out_specs=[VMEM] * len(chunks),
        scratch_shapes=[pltpu.VMEM((tokens, width), BF16)] * 2 + [pltpu.SemaphoreType.DMA((2,))],
        compiler_params=params(),
        name="pack_keys",
    )(*fixed(key_rows, value_rows), x_own[0])
    x_own += [queries_of(c, chunks[c], kv_own[0]) for c in range(1, len(chunks))]
    x_far = [send(x, across) for x in x_own]
    kv_level = [send(kv, level_in) for kv in kv_own]
    x_core = [send(x, core) for x in x_own]

    def work_of(heads):
        return 10 * tokens * tokens * 256 * heads

    def near(swapped, xs, dq_type, share):
        out = []
        for heads in chunks:
            rows = heads * head_dim
            out += [shape(rows, dq_type), shape(2 * rows, F32)]
        got = pl.pallas_call(
            functools.partial(near_kernel, chunks, head_dim, factor, count, swapped),
            out_shape=out,
            in_specs=[SMEM] * 2 + [VMEM] * (2 * len(chunks)),
            out_specs=[VMEM] * len(out),
            compiler_params=params(),
            cost_estimate=cost(int(work_of(HEADS) * share), 1024),
            name="near_tasks",
        )(keep_tasks, place, *xs, *kv_own)
        return got[::2], got[1::2]

    def far(c, level, x, hop, keys, earlier):
        rows = chunks[c] * head_dim
        dq_type = BF16 if earlier else F32
        return pl.pallas_call(
            functools.partial(far_kernel, chunks[c], head_dim, factor, count, level, not earlier),
            out_shape=[shape(rows, dq_type)] * 2 + [shape(2 * rows, BF16 if level else F32)],
            in_specs=[SMEM] * 2 + [VMEM] * (2 + HOPS + len(earlier)),
            out_specs=[VMEM] * 3,
            scratch_shapes=[pltpu.VMEM((2 * rows, tokens), F32)],
            compiler_params=params(),
            cost_estimate=cost(int(work_of(chunks[c]) * FAR_COST), 1024),
            name="far_tasks",
        )(keep_tasks, place, x, *hop, keys, *earlier)

    done = x_core[0]
    far_out = []
    for c in range(len(chunks)):
        x = after(x_far[c], done)
        hop = [send(piece, core) for piece in pl.pallas_call(
            split_kernel,
            out_shape=[
                pltpu.VMEM((chunks[c] * head_dim, tokens), BF16),
                pltpu.VMEM((x.shape[0] - chunks[c] * head_dim, tokens), BF16),
            ],
            in_specs=[VMEM],
            out_specs=[VMEM] * HOPS,
            compiler_params=params(),
            cost_estimate=cost(1024, 1024),
            name="split",
        )(x)]
        dq_x, dq_c, dkv_far = far(c, False, x, hop, kv_own[c], ())
        z = after(kv_level[c], dq_x)
        dq_x, dq_c, zdkv = far(c, True, x, hop, z, (dq_x, dq_c))
        done = dq_x
        dq_far = (dq_x.astype(F32) + send(dq_c, core).astype(F32)).astype(BF16)
        far_out.append((send(dq_far, across), dkv_far, send(zdkv, level_out)))
    dq_core, dkv_core = near(True, [after(value, done) for value in x_core], BF16, CORE_COST)
    done = dq_core[0]
    dq_own, dkv_own = near(False, [after(x, done, far_out[0][2]) for x in x_own], F32, SELF_COST)
    out = ()
    any_space = pl.BlockSpec(memory_space=pl.ANY)
    for c, heads in enumerate(chunks):
        rows = heads * head_dim
        dq_far, dkv_far, zdkv = far_out[c]
        args = (dq_own[c], send(dq_core[c], core), dq_far, dkv_own[c], dkv_core[c], dkv_far, zdkv)
        out = pl.pallas_call(
            functools.partial(finish_kernel, sum(chunks[:c]), heads, head_dim, scale),
            out_shape=[jax.ShapeDtypeStruct((tokens, width), BF16)] * 3,
            in_specs=[VMEM] * 7 + [any_space] * len(out),
            out_specs=[any_space] * 3,
            scratch_shapes=[pltpu.VMEM((tokens, rows), BF16)] * 3 + [pltpu.SemaphoreType.DMA((3,))],
            input_output_aliases={7 + i: i for i in range(len(out))},
            compiler_params=params(),
            cost_estimate=cost(1024, 1024),
            name="finish",
        )(*args, *out)
    return tuple(out)


def solution(mesh):
    rows = P(("groups", "tok"), None)
    return jax.shard_map(
        per_device,
        mesh=mesh,
        in_specs=(rows, rows, rows, rows, rows, P(None, ("groups", "tok")), P("groups", None)),
        out_specs=(rows, rows, rows),
        check_vma=False,
    )
```
